32 devices in a mesh: dp: 16 (over z, y, x), section: 2 (over core).
Axes of the slice: x: 2, y: 2, z: 4, core: 2. Of those that a mesh axis runs over, the one named last changes fastest.
Arguments:
- acts: bfloat16 [2, 32, 256, 512], P('section', 'dp'), may hold values from -6 to 6
- present: int32 [32], P('dp'), may hold values 0 or 1
- embed: bfloat16 [32, 2048], P('dp'), may hold values from -6 to 6
- context: bfloat16 [32, 4, 512], P('dp'), may hold values from -6 to 6
- norm1_gain: float32 [2, 512], P('section'), may hold values from 0.25 to 1.75
- norm1_bias: float32 [2, 512], P('section'), may hold values from -3 to 3
- conv1_weight: bfloat16 [2, 4608, 512], P('section'), may hold values from -0.09375 to 0.09375
- conv1_bias: float32 [2, 512], P('section'), may hold values from -3 to 3
- emb_weight: bfloat16 [2, 2048, 1024], P('section'), may hold values from -0.125 to 0.125
- emb_bias: float32 [2, 1024], P('section'), may hold values from -3 to 3
- norm2_gain: float32 [2, 512], P('section'), may hold values from 0.25 to 1.75
- norm2_bias: float32 [2, 512], P('section'), may hold values from -3 to 3
- conv2_weight: bfloat16 [2, 4608, 512], P('section'), may hold values from -0.09375 to 0.09375
- conv2_bias: float32 [2, 512], P('section'), may hold values from -3 to 3
- norm3_gain: float32 [2, 512], P('section'), may hold values from 0.25 to 1.75
- norm3_bias: float32 [2, 512], P('section'), may hold values from -3 to 3
- qkv_weight: bfloat16 [2, 512, 1536], P('section'), may hold values from -0.25 to 0.25
- context_weight: bfloat16 [2, 512, 1024], P('section'), may hold values from -0.25 to 0.25
- out_weight: bfloat16 [2, 512, 512], P('section'), may hold values from -1 to 1
- out_bias: float32 [2, 512], P('section'), may hold values from -3 to 3
Outputs:
- result: float32 [2, 32, 256, 512], P('section', 'dp')
- grad_norm1_gain: float32 [2, 512], P('section', 'dp')
- grad_norm1_bias: float32 [2, 512], P('section', 'dp')
- grad_conv1_weight: float32 [2, 4608, 512], P('section', 'dp')
- grad_conv1_bias: float32 [2, 512], P('section', 'dp')
- grad_emb_weight: float32 [2, 2048, 1024], P('section', 'dp')
- grad_emb_bias: float32 [2, 1024], P('section', 'dp')
- grad_norm2_gain: float32 [2, 512], P('section', 'dp')
- grad_norm2_bias: float32 [2, 512], P('section', 'dp')
- grad_conv2_weight: float32 [2, 4608, 512], P('section', 'dp')
- grad_conv2_bias: float32 [2, 512], P('section', 'dp')
- grad_norm3_gain: float32 [2, 512], P('section', 'dp')
- grad_norm3_bias: float32 [2, 512], P('section', 'dp')
- grad_qkv_weight: float32 [2, 512, 1536], P('section', 'dp')
- grad_context_weight: float32 [2, 512, 1024], P('section', 'dp')
- grad_out_weight: float32 [2, 512, 512], P('section', 'dp')
- grad_out_bias: float32 [2, 512], P('section', 'dp')
The draws below stay inside these ranges and needn't reach their ends.
All inputs are finite; a program needn't handle non-finite values. No bound on the sum of `present` on one device may be relied on, other than what follows from the above.
Results may differ from the reference program's by a relative error of at most 0.017.
Values may be sent and summed in bfloat16 or wider, within the bound.
No kernel may reach another device: no remote copies, remote signals or barrier semaphores. Data moves between devices by JAX's collectives and lax.ppermute only.
A program may use at most 448 MiB of HBM per device.

```python
import jax
import jax.numpy as jnp
from jax import lax

CH = 512
HEADS = 8
HEAD = 64
GROUPS = 32
EMB = 2048
CTX = 4
IMG = 16
PIX = 256
IMG_DEV = 2
IMAGES = 32


def touch_ends(array, own_key, least, largest):
    spot = [jax.random.randint(jax.random.fold_in(own_key, axis), (), 0, length) for axis, length in enumerate(array.shape)]
    longest = array.shape.index(max(array.shape))
    neighbour = spot[:longest] + [(spot[longest] + 1) % array.shape[longest]] + spot[longest + 1:]
    return array.at[tuple(spot)].set(least).at[tuple(neighbour)].set(largest)


def level_of(own_key, shape, cuts, smallest, high):
    loudness, own = 1.0, jax.random.fold_in(own_key, 6)
    for axis_at, shards_of in cuts:
        steps = jnp.exp(jax.random.uniform(jax.random.fold_in(own, axis_at), (shards_of,), jnp.float32, smallest / len(cuts), high / len(cuts)))
        loudness = loudness * jnp.repeat(steps, shape[axis_at] // shards_of).reshape([-1 if axis == axis_at else 1 for axis in range(len(shape))])
    return loudness


def scatter_about(stream_key, dims, scale, most, cuts=(), held_as=jnp.bfloat16):
    gain = level_of(stream_key, dims, cuts, -0.22, 0.18) if cuts else 1.0
    values = jax.random.normal(stream_key, dims, jnp.float32) * scale * gain
    return jnp.minimum(jnp.maximum(values, -most), most).astype(held_as)


def setup_inputs(seed: int = 0) -> dict:
    key_list = jax.random.split(jax.random.key(seed), 21)
    return {
        "acts": scatter_about(key_list[0], (2, IMAGES, PIX, CH), 1.0, 6.0, ((0, 2), (1, 16))),
        "present": touch_ends((jax.random.randint(key_list[1], (IMAGES,), 0, 4) < 3).astype(jnp.int32), jax.random.fold_in(key_list[1], 1), 0, 1),
        "embed": scatter_about(key_list[2], (IMAGES, EMB), 1.0, 6.0, ((0, 16),)),
        "context": scatter_about(key_list[3], (IMAGES, CTX, CH), 1.0, 6.0, ((0, 16),)),
        "norm1_gain": jnp.clip(1.0 + 0.15 * jax.random.normal(key_list[4], (2, CH), jnp.float32), 0.25, 1.75),
        "norm1_bias": scatter_about(key_list[5], (2, CH), 0.3, 3.0, ((0, 2),), jnp.float32),
        "conv1_weight": scatter_about(key_list[6], (2, 9 * CH, CH), (9 * CH) ** -0.5, 0.09375, ((0, 2),)),
        "conv1_bias": scatter_about(key_list[7], (2, CH), 0.3, 3.0, ((0, 2),), jnp.float32),
        "emb_weight": scatter_about(key_list[8], (2, EMB, 2 * CH), EMB ** -0.5, 0.125, ((0, 2),)),
        "emb_bias": scatter_about(key_list[9], (2, 2 * CH), 0.3, 3.0, ((0, 2),), jnp.float32),
        "norm2_gain": jnp.clip(1.0 + 0.15 * jax.random.normal(key_list[10], (2, CH), jnp.float32), 0.25, 1.75),
        "norm2_bias": scatter_about(key_list[11], (2, CH), 0.3, 3.0, ((0, 2),), jnp.float32),
        "conv2_weight": scatter_about(key_list[12], (2, 9 * CH, CH), (9 * CH) ** -0.5, 0.09375, ((0, 2),)),
        "conv2_bias": scatter_about(key_list[13], (2, CH), 0.3, 3.0, ((0, 2),), jnp.float32),
        "norm3_gain": jnp.clip(1.0 + 0.15 * jax.random.normal(key_list[14], (2, CH), jnp.float32), 0.25, 1.75),
        "norm3_bias": scatter_about(key_list[15], (2, CH), 0.3, 3.0, ((0, 2),), jnp.float32),
        "qkv_weight": scatter_about(key_list[16], (2, CH, 3 * CH), CH ** -0.5, 0.25, ((0, 2),)),
        "context_weight": scatter_about(key_list[17], (2, CH, 2 * CH), CH ** -0.5, 0.25, ((0, 2),)),
        "out_weight": scatter_about(key_list[18], (2, CH, CH), (CH // 16) ** -0.5, 1.0, ((0, 2),)),
        "out_bias": scatter_about(key_list[19], (2, CH), 0.3, 3.0, ((0, 2),), jnp.float32),
    }


PRECISE = lax.Precision.HIGHEST
EPSILON = 1e-05

@jax.custom_vjp
def low(v):
    return lax.optimization_barrier(v.astype(jnp.bfloat16)).astype(jnp.float32)

@jax.custom_vjp
def low_back(v):
    return v

def low_keep(v):
    return (low(v), None)

def low_pass(kept, grad):
    return (grad,)

def back_keep(v):
    return (v, None)

def back_low(kept, grad):
    return (low(grad),)
low.defvjp(low_keep, low_pass)
low_back.defvjp(back_keep, back_low)

def silu_of(values):
    return values * jax.nn.sigmoid(values)

def matmul(left, right):
    return jnp.dot(left, right, precision=PRECISE, preferred_element_type=jnp.float32)

def group_norm(values, scaling, offset):
    number, pixels, channels = values.shape
    grouped = values.reshape(number, pixels, GROUPS, channels // GROUPS)
    average = lax.optimization_barrier(jnp.mean(grouped, axis=(1, 3), keepdims=True))
    centered = grouped - average
    variance = lax.optimization_barrier(jnp.mean(centered * centered, axis=(1, 3), keepdims=True))
    return (centered * lax.rsqrt(variance + EPSILON)).reshape(values.shape) * scaling + offset

def patches_of(field_in):
    number, pixels, channels = field_in.shape
    grid_view = field_in.reshape(number, IMG, IMG, channels)
    padded = jnp.pad(grid_view, ((0, 0), (1, 1), (1, 1), (0, 0)))
    pieces = [padded[:, row_off:row_off + IMG, col_off:col_off + IMG, :] for row_off in range(3) for col_off in range(3)]
    return jnp.concatenate(pieces, axis=3).reshape(number * pixels, 9 * channels)

def decoder_layer(inputs, embed_g, context_g, weights):
    norm1_gain, norm1_bias, conv1_weight, conv1_bias, emb_weight, emb_bias, norm2_gain, norm2_bias, conv2_weight, conv2_bias, norm3_gain, norm3_bias, qkv_weight, context_weight, out_weight, out_bias = weights
    number, pixels, channels = inputs.shape
    first_act = low(silu_of(group_norm(inputs, norm1_gain, norm1_bias)))
    hidden = low_back(matmul(patches_of(first_act), conv1_weight).reshape(number, pixels, channels) + conv1_bias)
    modulation = low_back(matmul(low(silu_of(embed_g)), emb_weight) + emb_bias)
    normed_two = group_norm(hidden, norm2_gain, norm2_bias)
    second_act = low(silu_of(normed_two * (1.0 + modulation[:, None, :channels]) + modulation[:, None, channels:]))
    branch = low_back(matmul(patches_of(second_act), conv2_weight).reshape(number, pixels, channels) + conv2_bias)
    residual = inputs + branch
    normed = low(group_norm(residual, norm3_gain, norm3_bias))
    triple = low_back(low(matmul(normed.reshape(number * pixels, channels), qkv_weight)))
    triple = triple.reshape(number, pixels, 3 * channels)
    extra_kv = low_back(low(jnp.einsum('snc,cd->snd', context_g, context_weight, precision=PRECISE)))
    queries = triple[:, :, :channels].reshape(number, pixels, HEADS, HEAD)
    key_rows = jnp.concatenate([triple[:, :, channels:2 * channels], extra_kv[:, :, :channels]], axis=1)
    value_rows = jnp.concatenate([triple[:, :, 2 * channels:], extra_kv[:, :, channels:]], axis=1)
    key_rows = key_rows.reshape(number, key_rows.shape[1], HEADS, HEAD)
    value_rows = value_rows.reshape(number, value_rows.shape[1], HEADS, HEAD)
    scores = low_back(jnp.einsum('sqhd,skhd->shqk', queries, key_rows, precision=PRECISE) * HEAD ** (-0.5))
    highest = lax.optimization_barrier(jnp.max(scores, axis=-1, keepdims=True))
    expo = jnp.exp(scores - highest)
    probs = low(expo / lax.optimization_barrier(jnp.sum(expo, axis=-1, keepdims=True)))
    attended = low_back(low(jnp.einsum('shqk,skhd->sqhd', probs, value_rows, precision=PRECISE)))
    attended = attended.reshape(number * pixels, channels)
    projected = low_back(matmul(attended, out_weight).reshape(number, pixels, channels) + out_bias)
    return residual + projected

def reference(acts, present, embed, context, norm1_gain, norm1_bias, conv1_weight, conv1_bias, emb_weight, emb_bias, norm2_gain, norm2_bias, conv2_weight, conv2_bias, norm3_gain, norm3_bias, qkv_weight, context_weight, out_weight, out_bias):
    weight_args = (norm1_gain, norm1_bias, conv1_weight, conv1_bias, emb_weight, emb_bias, norm2_gain, norm2_bias, conv2_weight, conv2_bias, norm3_gain, norm3_bias, qkv_weight, context_weight, out_weight, out_bias)
    section_zero = tuple((weight_arg[0].astype(jnp.float32) for weight_arg in weight_args))
    section_one = tuple((weight_arg[1].astype(jnp.float32) for weight_arg in weight_args))
    group_size = IMG_DEV * 4
    group_count = IMAGES // group_size
    inputs_all = acts[0].astype(jnp.float32).reshape(group_count, group_size, PIX, CH)
    cotan_all = acts[1].astype(jnp.float32).reshape(group_count, group_size, PIX, CH)
    mask_all = present.astype(jnp.float32).reshape(group_count, group_size)
    embed_all = embed.astype(jnp.float32).reshape(group_count, group_size, EMB)
    context_all = context.astype(jnp.float32).reshape(group_count, group_size, CTX, CH)

    def one_group(running, group_in):
        inputs, cotan, mask_f, embed_g, context_g = group_in

        def full_model(inputs, params_zero, params_one):
            first_out = decoder_layer(inputs, embed_g, context_g, params_zero)
            passed = low_back(low(first_out + inputs))
            return decoder_layer(passed, embed_g, context_g, params_one) * mask_f[:, None, None]
        output, pullback = jax.vjp(full_model, inputs, section_zero, section_one)
        grad_in, grads_zero, grads_one = pullback(cotan)
        running = jax.tree.map(lambda acc_a, add_b: acc_a + add_b, running, (grads_zero, grads_one))
        return (running, (grad_in, output))
    start = (tuple((jnp.zeros(weight_arg.shape, jnp.float32) for weight_arg in section_zero)), tuple((jnp.zeros(weight_arg.shape, jnp.float32) for weight_arg in section_one)))
    totals, (grad_in, output) = lax.scan(one_group, start, (inputs_all, cotan_all, mask_all, embed_all, context_all))
    result = jnp.stack([grad_in.reshape(IMAGES, PIX, CH), output.reshape(IMAGES, PIX, CH)])
    grads = tuple((jnp.stack([grad_zero, grad_one]) for grad_zero, grad_one in zip(totals[0], totals[1])))
    return (result, grads[0], grads[1], grads[2], grads[3], grads[4], grads[5], grads[6], grads[7], grads[8], grads[9], grads[10], grads[11], grads[12], grads[13], grads[14], grads[15])
```

```python
import jax
import jax.numpy as jnp
from jax import lax
from jax.sharding import PartitionSpec as P

HEADS = 8
HEAD = 64
GROUPS = 32
IMG = 16
MB = 2


EPSILON = 1e-05


def passed_along(value, axis, steps):
    count = lax.axis_size(axis)
    first, last = (max(0, -steps), min(count, count - steps))
    return lax.ppermute(value, axis, [(source, source + steps) for source in range(first, last)])


def silu_of(values):
    return values * jax.nn.sigmoid(values)


def matmul(left, right):
    return jnp.dot(left, right, preferred_element_type=jnp.float32)


def outer_sum(left, right):
    return lax.dot_general(
        left, right, (((0,), (0,)), ((), ())), preferred_element_type=jnp.float32
    )


def times_transposed(left, right):
    return lax.dot_general(
        left, right, (((1,), (1,)), ((), ())), preferred_element_type=jnp.float32
    )


def group_norm(values, scaling, offset):
    number, pixels, channels = values.shape
    grouped = values.reshape(number, pixels, GROUPS, channels // GROUPS)
    average = jnp.mean(grouped, axis=(1, 3), keepdims=True)
    centered = grouped - average
    variance = jnp.mean(centered * centered, axis=(1, 3), keepdims=True)
    return (centered * lax.rsqrt(variance + EPSILON)).reshape(values.shape) * scaling + offset


def front_piece(inputs, scaling, offset):
    return silu_of(group_norm(inputs, scaling, offset))


def middle_piece(hidden, scaling, offset, modulation):
    channels = hidden.shape[2]
    normed = group_norm(hidden, scaling, offset)
    return silu_of(normed * (1.0 + modulation[:, None, :channels]) + modulation[:, None, channels:])


def patches_of(field_in):
    number, pixels, channels = field_in.shape
    grid_view = field_in.reshape(number, IMG, IMG, channels)
    padded = jnp.pad(grid_view, ((0, 0), (1, 1), (1, 1), (0, 0)))
    pieces = [
        padded[:, row_off : row_off + IMG, col_off : col_off + IMG, :]
        for row_off in range(3)
        for col_off in range(3)
    ]
    return jnp.concatenate(pieces, axis=3).reshape(number * pixels, 9 * channels)


def unpatch(grad_patch, number, pixels, channels):
    unused_out, pullback = jax.vjp(patches_of, jnp.zeros((number, pixels, channels), jnp.float32))
    return pullback(grad_patch)[0]


def heads_of(triple, extra_kv):
    number, pixels, triple_width = triple.shape
    channels = triple_width // 3
    queries = triple[:, :, :channels].reshape(number, pixels, HEADS, HEAD)
    key_rows = jnp.concatenate(
        [triple[:, :, channels : 2 * channels], extra_kv[:, :, :channels]], axis=1
    )
    value_rows = jnp.concatenate([triple[:, :, 2 * channels :], extra_kv[:, :, channels:]], axis=1)
    key_rows = key_rows.reshape(number, key_rows.shape[1], HEADS, HEAD)
    value_rows = value_rows.reshape(number, value_rows.shape[1], HEADS, HEAD)
    return (queries, key_rows, value_rows)


def attn_scores(queries, key_rows):
    return jnp.einsum(
        "sqhd,skhd->shqk", queries, key_rows, preferred_element_type=jnp.float32
    ) * HEAD ** (-0.5)


def forward_layer(inputs, embed_m, context_m, weights):
    (
        norm1_gain,
        norm1_bias,
        conv1_weight,
        conv1_bias,
        emb_weight,
        emb_bias,
        norm2_gain,
        norm2_bias,
        conv2_weight,
        conv2_bias,
        norm3_gain,
        norm3_bias,
        qkv_weight,
        context_weight,
        out_weight,
        out_bias,
    ) = weights
    number, pixels, channels = inputs.shape
    first_act = front_piece(inputs, norm1_gain, norm1_bias).astype(jnp.bfloat16)
    hidden = (
        matmul(patches_of(first_act), conv1_weight).reshape(number, pixels, channels) + conv1_bias
    )
    emb_act = silu_of(embed_m.astype(jnp.float32)).astype(jnp.bfloat16)
    modulation = matmul(emb_act, emb_weight) + emb_bias
    second_act = middle_piece(hidden, norm2_gain, norm2_bias, modulation).astype(jnp.bfloat16)
    branch = (
        matmul(patches_of(second_act), conv2_weight).reshape(number, pixels, channels) + conv2_bias
    )
    residual = inputs + branch
    normed = group_norm(residual, norm3_gain, norm3_bias).astype(jnp.bfloat16)
    triple = matmul(normed.reshape(number * pixels, channels), qkv_weight).astype(jnp.bfloat16)
    triple = triple.reshape(number, pixels, 3 * channels)
    extra_kv = jnp.einsum(
        "snc,cd->snd", context_m, context_weight, preferred_element_type=jnp.float32
    ).astype(jnp.bfloat16)
    queries, key_rows, value_rows = heads_of(triple, extra_kv)
    scores = attn_scores(queries, key_rows)
    highest = jnp.max(scores, axis=-1, keepdims=True)
    log_total = highest + jnp.log(jnp.sum(jnp.exp(scores - highest), axis=-1, keepdims=True))
    prob_b = jnp.exp(scores - log_total).astype(jnp.bfloat16)
    attended = jnp.einsum("shqk,skhd->sqhd", prob_b, value_rows, preferred_element_type=jnp.float32)
    attended = attended.astype(jnp.bfloat16).reshape(number * pixels, channels)
    projected = matmul(attended, out_weight).reshape(number, pixels, channels) + out_bias
    saved_list = (
        inputs,
        first_act,
        hidden,
        emb_act,
        modulation,
        second_act,
        residual,
        normed,
        triple,
        extra_kv,
        log_total,
        attended,
    )
    return (residual + projected, saved_list)


def blank_saved(number, pixels, channels, emb_width, extra_count):
    bf16 = jnp.bfloat16
    f32 = jnp.float32
    return (
        jnp.zeros((number, pixels, channels), f32),
        jnp.zeros((number, pixels, channels), bf16),
        jnp.zeros((number, pixels, channels), f32),
        jnp.zeros((number, emb_width), bf16),
        jnp.zeros((number, 2 * channels), f32),
        jnp.zeros((number, pixels, channels), bf16),
        jnp.zeros((number, pixels, channels), f32),
        jnp.zeros((number, pixels, channels), bf16),
        jnp.zeros((number, pixels, 3 * channels), bf16),
        jnp.zeros((number, extra_count, 2 * channels), bf16),
        jnp.zeros((number, HEADS, pixels, 1), f32),
        jnp.zeros((number * pixels, channels), bf16),
    )


def backward_layer(saved_list, grad_out, context_m, weights):
    (
        norm1_gain,
        norm1_bias,
        conv1_weight,
        conv1_bias,
        emb_weight,
        emb_bias,
        norm2_gain,
        norm2_bias,
        conv2_weight,
        conv2_bias,
        norm3_gain,
        norm3_bias,
        qkv_weight,
        context_weight,
        out_weight,
        out_bias,
    ) = weights
    (
        inputs,
        first_act,
        hidden,
        emb_act,
        modulation,
        second_act,
        residual,
        normed,
        triple,
        extra_kv,
        log_total,
        attended,
    ) = saved_list
    number, pixels, channels = inputs.shape
    grad_b = grad_out.astype(jnp.bfloat16).reshape(number * pixels, channels)
    g_out_weight = outer_sum(attended, grad_b)
    g_out_bias = jnp.sum(grad_b.astype(jnp.float32), axis=0)
    d_att = (
        times_transposed(grad_b, out_weight)
        .astype(jnp.bfloat16)
        .reshape(number, pixels, HEADS, HEAD)
    )
    queries, key_rows, value_rows = heads_of(triple, extra_kv)
    prob_f = jnp.exp(attn_scores(queries, key_rows) - log_total)
    prob_b = prob_f.astype(jnp.bfloat16)
    d_probs = jnp.einsum("sqhd,skhd->shqk", d_att, value_rows, preferred_element_type=jnp.float32)
    row_dot = jnp.sum(prob_f * d_probs, axis=-1, keepdims=True)
    d_scores = (prob_f * (d_probs - row_dot)).astype(jnp.bfloat16)
    d_queries = jnp.einsum(
        "shqk,skhd->sqhd", d_scores, key_rows, preferred_element_type=jnp.float32
    ) * HEAD ** (-0.5)
    d_keys = jnp.einsum(
        "shqk,sqhd->skhd", d_scores, queries, preferred_element_type=jnp.float32
    ) * HEAD ** (-0.5)
    d_values = jnp.einsum("shqk,sqhd->skhd", prob_b, d_att, preferred_element_type=jnp.float32)
    extra_count = extra_kv.shape[1]
    d_triple = jnp.concatenate(
        [
            d_queries.reshape(number, pixels, channels),
            d_keys[:, :pixels].reshape(number, pixels, channels),
            d_values[:, :pixels].reshape(number, pixels, channels),
        ],
        axis=2,
    ).astype(jnp.bfloat16)
    d_extra = jnp.concatenate(
        [
            d_keys[:, pixels:].reshape(number, extra_count, channels),
            d_values[:, pixels:].reshape(number, extra_count, channels),
        ],
        axis=2,
    ).astype(jnp.bfloat16)
    d_triple = d_triple.reshape(number * pixels, 3 * channels)
    g_qkv = outer_sum(normed.reshape(number * pixels, channels), d_triple)
    d_normed = times_transposed(d_triple, qkv_weight).reshape(number, pixels, channels)
    unused_three, pull_three = jax.vjp(group_norm, residual, norm3_gain, norm3_bias)
    d_resid_add, g_norm3_gain, g_norm3_bias = pull_three(d_normed)
    d_resid = grad_out + d_resid_add
    d_branch = d_resid.astype(jnp.bfloat16).reshape(number * pixels, channels)
    g_conv2 = outer_sum(patches_of(second_act), d_branch)
    g_conv2_bias = jnp.sum(d_branch.astype(jnp.float32), axis=0)
    d_second = unpatch(times_transposed(d_branch, conv2_weight), number, pixels, channels)
    unused_two, pull_two = jax.vjp(middle_piece, hidden, norm2_gain, norm2_bias, modulation)
    d_hidden, g_norm2_gain, g_norm2_bias, d_modul = pull_two(d_second)
    d_modul_b = d_modul.astype(jnp.bfloat16)
    d_hidden_b = d_hidden.astype(jnp.bfloat16).reshape(number * pixels, channels)
    g_conv1 = outer_sum(patches_of(first_act), d_hidden_b)
    g_conv1_bias = jnp.sum(d_hidden_b.astype(jnp.float32), axis=0)
    d_first = unpatch(times_transposed(d_hidden_b, conv1_weight), number, pixels, channels)
    unused_one, pull_one = jax.vjp(front_piece, inputs, norm1_gain, norm1_bias)
    d_in_add, g_norm1_gain, g_norm1_bias = pull_one(d_first)
    grads = (
        g_norm1_gain,
        g_norm1_bias,
        g_conv1,
        g_conv1_bias,
        g_norm2_gain,
        g_norm2_bias,
        g_conv2,
        g_conv2_bias,
        g_norm3_gain,
        g_norm3_bias,
        g_qkv,
        g_out_weight,
        g_out_bias,
    )
    return (d_resid + d_in_add, grads, d_modul_b, d_extra)


def halved_sums(arrays, axis):
    count = lax.axis_size(axis)
    index = lax.axis_index(axis)
    bits = [1 << k for k in range(count.bit_length() - 1)]
    orders = (bits, bits[1::-1] + bits[2:], bits[2:] + bits[:2])
    state = []
    for number, array in enumerate(arrays):
        state.append((array, bits, orders[number % 3]))
    for step in range(len(bits)):
        held = []
        for array, left, order in state:
            bit = order[step]
            above = len([one for one in left if one > bit])
            view = array.reshape((1 << above, 2, array.shape[0] >> (above + 1)) + array.shape[1:])
            mine = (index // bit) % 2
            keep = lax.dynamic_index_in_dim(view, mine, 1, keepdims=False)
            send = lax.dynamic_index_in_dim(view, 1 - mine, 1, keepdims=False).astype(jnp.bfloat16)
            got = lax.ppermute(send, axis, [(one, one ^ bit) for one in range(count)])
            held.append((keep, got, [one for one in left if one != bit], order))
        state = [
            ((keep + got.astype(jnp.float32)).reshape((-1,) + keep.shape[2:]), left, order)
            for keep, got, left, order in held
        ]
    return [array[0] for array, left, order in state]


def two_parts(values):
    high = values.astype(jnp.bfloat16)
    return jnp.concatenate([high, (values - high.astype(jnp.float32)).astype(jnp.bfloat16)], axis=1)


def body(
    acts,
    present,
    embed,
    context,
    norm1_gain,
    norm1_bias,
    conv1_weight,
    conv1_bias,
    emb_weight,
    emb_bias,
    norm2_gain,
    norm2_bias,
    conv2_weight,
    conv2_bias,
    norm3_gain,
    norm3_bias,
    qkv_weight,
    context_weight,
    out_weight,
    out_bias,
):
    weights = tuple(
        (
            weight_arg[0]
            for weight_arg in (
                norm1_gain,
                norm1_bias,
                conv1_weight,
                conv1_bias,
                emb_weight,
                emb_bias,
                norm2_gain,
                norm2_bias,
                conv2_weight,
                conv2_bias,
                norm3_gain,
                norm3_bias,
                qkv_weight,
                context_weight,
                out_weight,
                out_bias,
            )
        )
    )
    section_id = lax.axis_index("section")
    is_first = section_id == 0
    images_dev = acts.shape[1]
    pixels = acts.shape[2]
    channels = acts.shape[3]
    per_batch = images_dev // MB
    emb_width = embed.shape[1]
    extra_count = context.shape[1]
    mask_f = present.astype(jnp.float32)[:, None, None]
    source = acts[0].astype(jnp.float32)
    cotan = source * mask_f

    def pick(array, batch_idx):
        return lax.dynamic_slice_in_dim(array, batch_idx * per_batch, per_batch, 0)

    def zero_field():
        return jnp.zeros((per_batch, pixels, channels), jnp.float32)

    received = zero_field()
    outputs = jnp.zeros((images_dev, pixels, channels), jnp.float32)
    stash_list = []
    for step_now in range(MB + 1):
        batch_raw = step_now - section_id
        active = (batch_raw >= 0) & (batch_raw < MB)
        batch_idx = jnp.clip(batch_raw, 0, MB - 1)
        layer_in = jnp.where(is_first, pick(source, batch_idx), received)
        embed_m = pick(embed, batch_idx)
        context_m = pick(context, batch_idx)
        layer_out, saved_list = lax.cond(
            active,
            lambda field_in, embed_in, context_in: forward_layer(
                field_in, embed_in, context_in, weights
            ),
            lambda field_in, embed_in, context_in: (
                zero_field(),
                blank_saved(per_batch, pixels, channels, emb_width, extra_count),
            ),
            layer_in,
            embed_m,
            context_m,
        )
        stash_list.append(saved_list)
        if step_now < MB:
            sending = (layer_out + layer_in).astype(jnp.bfloat16)
            received = passed_along(sending, "section", 1).astype(jnp.float32)
        current = pick(outputs, batch_idx)
        outputs = lax.dynamic_update_slice_in_dim(
            outputs, jnp.where(active, layer_out, current), batch_idx * per_batch, 0
        )

    kept = [place for place in range(len(weights)) if place not in (4, 5, 13)]

    def zero_grads():
        return tuple((jnp.zeros(weights[place].shape, jnp.float32) for place in kept))

    back_recv = zero_field()
    grad_input = jnp.zeros((images_dev, pixels, channels), jnp.float32)
    totals = zero_grads()
    d_mod_all = jnp.zeros((images_dev, 2 * channels), jnp.bfloat16)
    d_extra_all = jnp.zeros((images_dev, extra_count, 2 * channels), jnp.bfloat16)
    for step_now in range(MB + 1):
        batch_raw = MB - step_now - section_id
        active = (batch_raw >= 0) & (batch_raw < MB)
        batch_idx = jnp.clip(batch_raw, 0, MB - 1)
        grad_out = jnp.where(is_first, back_recv, pick(cotan, batch_idx))
        embed_m = pick(embed, batch_idx)
        context_m = pick(context, batch_idx)
        stashed = stash_list[MB - step_now]
        d_inputs, grads, d_mod, d_extra = lax.cond(
            active,
            lambda saved_in, grad_in, embed_in, context_in: backward_layer(
                saved_in, grad_in, context_in, weights
            ),
            lambda saved_in, grad_in, embed_in, context_in: (
                zero_field(),
                zero_grads(),
                jnp.zeros((per_batch, 2 * channels), jnp.bfloat16),
                jnp.zeros((per_batch, extra_count, 2 * channels), jnp.bfloat16),
            ),
            stashed,
            grad_out,
            embed_m,
            context_m,
        )
        if step_now < MB:
            back_recv = passed_along(d_inputs.astype(jnp.bfloat16), "section", -1).astype(
                jnp.float32
            )
        current = pick(grad_input, batch_idx)
        grad_input = lax.dynamic_update_slice_in_dim(
            grad_input, jnp.where(active, d_inputs + grad_out, current), batch_idx * per_batch, 0
        )
        totals = tuple((acc_a + add_b for acc_a, add_b in zip(totals, grads)))
        d_mod_all = lax.dynamic_update_slice_in_dim(
            d_mod_all,
            jnp.where(active, d_mod, pick(d_mod_all, batch_idx)),
            batch_idx * per_batch,
            0,
        )
        d_extra_all = lax.dynamic_update_slice_in_dim(
            d_extra_all,
            jnp.where(active, d_extra, pick(d_extra_all, batch_idx)),
            batch_idx * per_batch,
            0,
        )
    count = lax.axis_size("dp")

    def by_shard(array):
        return array.reshape((count, array.shape[0] // count) + array.shape[1:])

    total_of = dict(zip(kept, totals))
    rest = jnp.concatenate(
        [by_shard(total_of[12]), by_shard(total_of[14])], axis=2
    )
    conv1_shard, conv2_shard, rest_shard = halved_sums(
        [by_shard(total_of[2]), by_shard(total_of[8]), rest], "dp"
    )
    vector_at = [place for place in kept if weights[place].ndim == 1]
    vectors = jnp.concatenate([by_shard(total_of[place]) for place in vector_at], axis=1)
    width = vectors.shape[1]
    wide = 2 * channels
    emb_act = silu_of(embed.astype(jnp.float32)).astype(jnp.bfloat16)
    emb_cols = emb_width // count
    context_cols = channels // count

    def split_columns(array, columns):
        return array.reshape(-1, count, columns).swapaxes(0, 1).reshape(count, -1)

    early = jnp.concatenate(
        [
            split_columns(emb_act, emb_cols),
            split_columns(context.reshape(-1, channels), context_cols),
        ],
        axis=1,
    )
    early = lax.all_to_all(early, "dp", 0, 0)
    emb_part = early[:, : images_dev * emb_cols].reshape(count * images_dev, emb_cols)
    context_part = early[:, images_dev * emb_cols :].reshape(-1, context_cols)
    same = jnp.concatenate([d_mod_all.reshape(-1), d_extra_all.reshape(-1)])
    late = jnp.concatenate(
        [two_parts(vectors), jnp.broadcast_to(same[None], (count, same.shape[0]))], axis=1
    )
    late = lax.all_to_all(late, "dp", 0, 0)
    summed = jnp.sum(late[:, : 2 * width].astype(jnp.float32), axis=0)
    summed = summed[:width] + summed[width:]
    d_mod_g = late[:, 2 * width : 2 * width + images_dev * wide].reshape(-1, wide)
    d_extra_g = late[:, 2 * width + images_dev * wide :].reshape(-1, wide)
    each = channels // count
    vector_of = {
        place: summed[number * each : (number + 1) * each]
        for number, place in enumerate(vector_at)
    }
    emb_bias_all = jnp.sum(d_mod_g.astype(jnp.float32), axis=0)
    emb_bias_shard = lax.dynamic_slice_in_dim(
        emb_bias_all, lax.axis_index("dp") * (wide // count), wide // count, 0
    )
    shard_of = dict(vector_of)
    shard_of[2] = conv1_shard
    shard_of[8] = conv2_shard
    shard_of[4] = outer_sum(emb_part, d_mod_g)
    shard_of[5] = emb_bias_shard
    shard_of[12] = rest_shard[:, : 3 * channels]
    shard_of[13] = outer_sum(context_part, d_extra_g)
    shard_of[14] = rest_shard[:, 3 * channels :]
    shards = [shard_of[place][None] for place in range(len(weights))]
    result = jnp.where(is_first, grad_input, outputs * mask_f)[None]
    return (result,) + tuple(shards)


def solution(mesh):
    in_specs = (
        P("section", "dp", None, None),
        P("dp"),
        P("dp", None),
        P("dp", None, None),
        P("section", None),
        P("section", None),
        P("section", None, None),
        P("section", None),
        P("section", None, None),
        P("section", None),
        P("section", None),
        P("section", None),
        P("section", None, None),
        P("section", None),
        P("section", None),
        P("section", None),
        P("section", None, None),
        P("section", None, None),
        P("section", None, None),
        P("section", None),
    )
    out_specs = (
        P("section", "dp", None, None),
        P("section", "dp"),
        P("section", "dp"),
        P("section", "dp", None),
        P("section", "dp"),
        P("section", "dp", None),
        P("section", "dp"),
        P("section", "dp"),
        P("section", "dp"),
        P("section", "dp", None),
        P("section", "dp"),
        P("section", "dp"),
        P("section", "dp"),
        P("section", "dp", None),
        P("section", "dp", None),
        P("section", "dp", None),
        P("section", "dp"),
    )
    return jax.shard_map(body, mesh=mesh, in_specs=in_specs, out_specs=out_specs, check_vma=False)
```

```python
import functools

import jax
import jax.numpy as jnp
from jax import lax
from jax.experimental import pallas as pl
from jax.experimental.pallas import tpu as pltpu
from jax.sharding import PartitionSpec as P

HEADS = 8
HEAD = 64
GROUPS = 32
IMG = 16
EPSILON = 1e-05
LANES = 128
EDGE = IMG
CTX_ROWS = 16
BF16 = jnp.bfloat16
F32 = jnp.float32
(N1G, N1B, C1B, N2G, N2B, C2B, N3G, N3B, OB, SCALE, SHIFT) = range(11)
VEC_ROWS = 16
NT = (((1,), (1,)), ((), ()))
TN = (((0,), (0,)), ((), ()))


def nn(left, right):
    return jnp.dot(left, right, preferred_element_type=F32)


def nt(left, right):
    return lax.dot_general(left, right, NT, preferred_element_type=F32)


def tn(left, right):
    return lax.dot_general(left, right, TN, preferred_element_type=F32)


def group_sum(rows):
    lane = lax.broadcasted_iota(jnp.int32, rows.shape, 1)
    for step in (1, 2, 4, 8):
        above = pltpu.roll(rows, LANES - step, 1)
        below = pltpu.roll(rows, step, 1)
        rows = rows + jnp.where((lane & step) != 0, below, above)
    return rows


def centre(block):
    count = block.shape[0] * 16
    mean = group_sum(jnp.sum(block, axis=0, keepdims=True)) * (1.0 / count)
    block = block - mean
    var = group_sum(jnp.sum(block * block, axis=0, keepdims=True)) * (1.0 / count)
    rstd = lax.rsqrt(var + EPSILON)
    return block * rstd, rstd


def sigmoid(values):
    return 1.0 / (1.0 + jnp.exp(-values))


def put_shifted(field, lanes, block):
    pixels, width = block.shape[0], field.shape[1] // 3
    column = lax.broadcasted_iota(jnp.int32, block.shape, 0) % IMG
    before = jnp.where(column == 0, 0.0, pltpu.roll(block, 1, 0))
    after = jnp.where(column == IMG - 1, 0.0, pltpu.roll(block, pixels - 1, 0))
    for place, one in enumerate((before, block, after)):
        field[EDGE : EDGE + pixels, place * width + lanes : place * width + lanes + LANES] = one.astype(BF16)


def clear_edges(field):
    zeros = jnp.zeros((EDGE, field.shape[1]), BF16)
    field[0:EDGE, :] = zeros
    field[field.shape[0] - EDGE :, :] = zeros


def conv_of(field, weight, lanes, wide, pixels):
    depth = weight.shape[0] // 3
    total = None
    for row in range(3):
        part = nn(
            field[row * IMG : row * IMG + pixels, :],
            weight[row * depth : (row + 1) * depth, lanes : lanes + wide],
        )
        total = part if total is None else total + part
    return total


def conv_back(field, weight, lanes, wide, pixels):
    width = weight.shape[1]
    total = None
    for row in range(3):
        for col in range(3):
            tap = (row * 3 + col) * width
            part = nt(
                field[(2 - row) * IMG : (2 - row) * IMG + pixels, (2 - col) * width : (3 - col) * width],
                weight[tap + lanes : tap + lanes + wide, :],
            )
            total = part if total is None else total + part
    return total


def loads(pairs, sems):
    copies = [pltpu.make_async_copy(src, dst, sems.at[n]) for n, (src, dst) in enumerate(pairs)]
    for copy in copies:
        copy.start()
    return copies


def forward_kernel(
    v_ref, vec, kvc, conv1_h, conv2_h, qkv_h, out_h,
    l_ref, send_ref, a1t, a2t, n3t, ot, h_ref, r_ref, qkv_ref, lse_ref,
    conv1, conv2, qkvw, outw, field, act, o_ref, sems,
):
    pixels, channels = v_ref.shape
    blocks = [slice(n, n + LANES) for n in range(0, channels, LANES)]
    waits = loads(((conv1_h, conv1), (conv2_h, conv2), (qkv_h, qkvw), (out_h, outw)), sems)
    clear_edges(field)
    for at in blocks:
        xhat, _ = centre(v_ref[:, at].astype(F32))
        u = xhat * vec[N1G : N1G + 1, at] + vec[N1B : N1B + 1, at]
        a1 = u * sigmoid(u)
        put_shifted(field, at.start, a1)
        a1t[at, :] = a1.astype(BF16).T
    waits[0].wait()
    wide = 2 * LANES
    for lanes in range(0, channels, wide):
        h_ref[:, lanes : lanes + wide] = (
            conv_of(field, conv1, lanes, wide, pixels) + vec[C1B : C1B + 1, lanes : lanes + wide]
        )
    for at in blocks:
        xhat, _ = centre(h_ref[:, at])
        n = xhat * vec[N2G : N2G + 1, at] + vec[N2B : N2B + 1, at]
        u = n * (1.0 + vec[SCALE : SCALE + 1, at]) + vec[SHIFT : SHIFT + 1, at]
        a2 = u * sigmoid(u)
        put_shifted(field, at.start, a2)
        a2t[at, :] = a2.astype(BF16).T
    waits[1].wait()
    for lanes in range(0, channels, wide):
        r_ref[:, lanes : lanes + wide] = (
            conv_of(field, conv2, lanes, wide, pixels) + vec[C2B : C2B + 1, lanes : lanes + wide]
        ) + v_ref[:, lanes : lanes + wide].astype(F32)
    for at in blocks:
        xhat, _ = centre(r_ref[:, at])
        n3 = (xhat * vec[N3G : N3G + 1, at] + vec[N3B : N3B + 1, at]).astype(BF16)
        act[:, at] = n3
        n3t[at, :] = n3.T
    waits[2].wait()
    for lanes in range(0, 3 * channels, wide):
        part = nn(act[...], qkvw[:, lanes : lanes + wide])
        if lanes < channels:
            part = part.astype(BF16).astype(F32) * HEAD ** (-0.5)
        qkv_ref[:, lanes : lanes + wide] = part.astype(BF16)
    lane = lax.broadcasted_iota(jnp.int32, (pixels, LANES), 1)
    token = lax.broadcasted_iota(jnp.int32, (CTX_ROWS, pixels), 0)
    zero = jnp.zeros((pixels, LANES), BF16)
    for pair, at in enumerate(blocks):
        at_v = slice(channels + at.start, channels + at.stop)
        q2 = qkv_ref[:, at]
        k2 = qkv_ref[:, channels + at.start : channels + at.stop]
        v2t = qkv_ref[:, 2 * channels + at.start : 2 * channels + at.stop].T
        kc, vc = kvc[:, at], kvc[:, at_v]
        for half in range(2):
            head = 2 * pair + half
            qm = jnp.where((lane >= HEAD) == (half == 1), q2, zero)
            s = nt(k2, qm)
            sc = jnp.where(token < kvc_tokens, nt(kc, qm), -jnp.inf)
            top = jnp.maximum(jnp.max(s, axis=0, keepdims=True), jnp.max(sc, axis=0, keepdims=True))
            e, ec = jnp.exp(s - top), jnp.exp(sc - top)
            total = jnp.sum(e, axis=0, keepdims=True) + jnp.sum(ec, axis=0, keepdims=True)
            lse_ref[head : head + 1, :] = top + jnp.log(total)
            share = 1.0 / total
            p, pc = (e * share).astype(BF16), (ec * share).astype(BF16)
            rows = slice(half * HEAD, (half + 1) * HEAD)
            o = nn(v2t[rows, :], p) + tn(vc, pc)[rows, :]
            ot[head * HEAD : (head + 1) * HEAD, :] = o.astype(BF16)
        o_ref[:, at] = ot[at, :].T
    waits[3].wait()
    for lanes in range(0, channels, wide):
        cols = slice(lanes, lanes + wide)
        layer = nn(o_ref[...], outw[:, cols]) + vec[OB : OB + 1, cols] + r_ref[:, cols]
        l_ref[:, cols] = layer
        send_ref[:, cols] = (layer + v_ref[:, cols].astype(F32)).astype(BF16)


kvc_tokens = 4


def forward_call(v, vec, kvc, conv1, conv2, qkv, out):
    pixels, channels = v.shape
    whole = pl.BlockSpec(memory_space=pltpu.VMEM)
    hbm = pl.BlockSpec(memory_space=pl.ANY)
    sds = jax.ShapeDtypeStruct
    tr = sds((channels, pixels), BF16)
    f = sds((pixels, channels), F32)
    return pl.pallas_call(
        forward_kernel,
        in_specs=[whole] * 3 + [hbm] * 4,
        out_specs=[whole] * 10,
        out_shape=[f, sds((pixels, channels), BF16), tr, tr, tr, tr, f, f, sds((pixels, 3 * channels), BF16), sds((HEADS, pixels), F32)],
        scratch_shapes=[pltpu.VMEM(w.shape, BF16) for w in (conv1, conv2, qkv, out)]
        + [pltpu.VMEM((pixels + 2 * EDGE, 3 * channels), BF16), pltpu.VMEM((pixels, channels), BF16), pltpu.VMEM((pixels, channels), BF16), pltpu.SemaphoreType.DMA((4,))],
        compiler_params=pltpu.CompilerParams(vmem_limit_bytes=48 << 20),
        name="forward_layer",
    )(v, vec, kvc, conv1, conv2, qkv, out)


(G_N1G, G_N1B, G_C1B, G_N2G, G_N2B, G_C2B, G_N3G, G_N3B, G_OB, G_SCALE, G_SHIFT) = range(11)


def norm_back(block, dy, gain, cast=None):
    xhat, rstd = centre(block)
    return scaled_back(xhat, rstd, dy, gain)


def scaled_back(xhat, rstd, dy, gain):
    count = xhat.shape[0] * 16
    d_gain = jnp.sum(dy * xhat, axis=0, keepdims=True)
    d_bias = jnp.sum(dy, axis=0, keepdims=True)
    both = group_sum(jnp.concatenate([d_bias * gain, d_gain * gain], axis=0)) * (1.0 / count)
    dx = rstd * (dy * gain - both[0:1] - xhat * both[1:2])
    return dx, d_gain, d_bias


def column_sum(block):
    return jnp.sum(block, axis=0, keepdims=True)


def backward_kernel(
    g_ref, v_ref, vec, kvc, h_ref, r_ref, qkv_ref, lse_ref, out_h, qkv_h, conv2_h, conv1_h,
    send_ref, res_ref, dqkv_ref, dkvc_ref, db_ref, dhb_ref, gv,
    outw, qkvw, conv2, conv1, field, d_o, dr, tmp, sems,
):
    pixels, channels = v_ref.shape
    blocks = [slice(n, n + LANES) for n in range(0, channels, LANES)]
    wide = 2 * LANES
    waits = loads(((out_h, outw), (qkv_h, qkvw), (conv2_h, conv2), (conv1_h, conv1)), sems)
    clear_edges(field)
    gv[...] = jnp.zeros(gv.shape, F32)
    for at in blocks:
        gv[G_OB : G_OB + 1, at] = column_sum(g_ref[:, at].astype(F32))
    waits[0].wait()
    for lanes in range(0, channels, wide):
        d_o[:, lanes : lanes + wide] = nt(g_ref[...], outw[lanes : lanes + wide, :]).astype(BF16)
    lane = lax.broadcasted_iota(jnp.int32, (pixels, LANES), 1)
    token = lax.broadcasted_iota(jnp.int32, (CTX_ROWS, pixels), 0)
    zero = jnp.zeros((pixels, LANES), BF16)
    for pair, at in enumerate(blocks):
        at_v = slice(channels + at.start, channels + at.stop)
        at_vv = slice(2 * channels + at.start, 2 * channels + at.stop)
        q2, do2 = qkv_ref[:, at], d_o[:, at]
        k2, v2 = qkv_ref[:, at_v], qkv_ref[:, at_vv]
        kc, vc = kvc[:, at], kvc[:, at_v]
        k2t = k2.T
        dk = dv = dkc = dvc = None
        dqt = []
        for half in range(2):
            head = 2 * pair + half
            mine = (lane >= HEAD) == (half == 1)
            qm, dom = jnp.where(mine, q2, zero), jnp.where(mine, do2, zero)
            lse = lse_ref[head : head + 1, :]
            p = jnp.exp(nt(k2, qm) - lse)
            pc = jnp.exp(jnp.where(token < kvc_tokens, nt(kc, qm), -jnp.inf) - lse)
            dp, dpc = nt(v2, dom), nt(vc, dom)
            dot = column_sum(p * dp) + column_sum(pc * dpc)
            ds, dsc = (p * (dp - dot)).astype(BF16), (pc * (dpc - dot)).astype(BF16)
            pb, pcb = p.astype(BF16), pc.astype(BF16)
            rows = slice(half * HEAD, (half + 1) * HEAD)
            dqt.append((nn(k2t[rows, :], ds) + tn(kc, dsc)[rows, :]) * HEAD ** (-0.5))
            parts = (nn(ds, qm), nn(pb, dom), nn(dsc, qm), nn(pcb, dom))
            if half == 0:
                dk, dv, dkc, dvc = parts
            else:
                dk, dv, dkc, dvc = dk + parts[0], dv + parts[1], dkc + parts[2], dvc + parts[3]
        dqkv_ref[:, at] = jnp.concatenate(dqt, axis=0).astype(BF16).T
        dqkv_ref[:, at_v] = dk.astype(BF16)
        dqkv_ref[:, at_vv] = dv.astype(BF16)
        dkvc_ref[:, at] = dkc.astype(BF16)
        dkvc_ref[:, at_v] = dvc.astype(BF16)
    waits[1].wait()
    for lanes in range(0, channels, wide):
        tmp[:, lanes : lanes + wide] = nt(dqkv_ref[...], qkvw[lanes : lanes + wide, :])
    for at in blocks:
        xhat, rstd = centre(r_ref[:, at])
        dx, d_gain, d_bias = scaled_back(xhat, rstd, tmp[:, at], vec[N3G : N3G + 1, at])
        gv[G_N3G : G_N3G + 1, at] = d_gain
        gv[G_N3B : G_N3B + 1, at] = d_bias
        total = g_ref[:, at].astype(F32) + dx
        dr[:, at] = total
        rounded = total.astype(BF16)
        db_ref[:, at] = rounded
        rounded = rounded.astype(F32)
        gv[G_C2B : G_C2B + 1, at] = column_sum(rounded)
        put_shifted(field, at.start, rounded)
    waits[2].wait()
    for lanes in range(0, channels, wide):
        tmp[:, lanes : lanes + wide] = conv_back(field, conv2, lanes, wide, pixels)
    for at in blocks:
        xhat, rstd = centre(h_ref[:, at])
        gain, bias = vec[N2G : N2G + 1, at], vec[N2B : N2B + 1, at]
        more = 1.0 + vec[SCALE : SCALE + 1, at]
        u = (xhat * gain + bias) * more + vec[SHIFT : SHIFT + 1, at]
        s = sigmoid(u)
        du = tmp[:, at] * (s * (1.0 + u * (1.0 - s)))
        dx, d_gain, d_bias = scaled_back(xhat, rstd, du, gain * more)
        gv[G_SHIFT : G_SHIFT + 1, at] = d_bias
        gv[G_SCALE : G_SCALE + 1, at] = d_gain * gain + d_bias * bias
        gv[G_N2G : G_N2G + 1, at] = d_gain * more
        gv[G_N2B : G_N2B + 1, at] = d_bias * more
        rounded = dx.astype(BF16)
        dhb_ref[:, at] = rounded
        rounded = rounded.astype(F32)
        gv[G_C1B : G_C1B + 1, at] = column_sum(rounded)
        put_shifted(field, at.start, rounded)
    waits[3].wait()
    for lanes in range(0, channels, wide):
        tmp[:, lanes : lanes + wide] = conv_back(field, conv1, lanes, wide, pixels)
    for at in blocks:
        xhat, rstd = centre(v_ref[:, at].astype(F32))
        gain = vec[N1G : N1G + 1, at]
        u = xhat * gain + vec[N1B : N1B + 1, at]
        s = sigmoid(u)
        du = tmp[:, at] * (s * (1.0 + u * (1.0 - s)))
        dx, d_gain, d_bias = scaled_back(xhat, rstd, du, gain)
        gv[G_N1G : G_N1G + 1, at] = d_gain
        gv[G_N1B : G_N1B + 1, at] = d_bias
        total = dr[:, at] + dx
        send_ref[:, at] = total.astype(BF16)
        res_ref[:, at] = total + g_ref[:, at].astype(F32)


def backward_call(g, v, vec, kvc, h, r, qkv_s, lse, out, qkv, conv2, conv1):
    pixels, channels = v.shape
    whole = pl.BlockSpec(memory_space=pltpu.VMEM)
    hbm = pl.BlockSpec(memory_space=pl.ANY)
    sds = jax.ShapeDtypeStruct
    b = sds((pixels, channels), BF16)
    f = sds((pixels, channels), F32)
    return pl.pallas_call(
        backward_kernel,
        in_specs=[whole] * 8 + [hbm] * 4,
        out_specs=[whole] * 7,
        out_shape=[b, f, sds((pixels, 3 * channels), BF16), sds((CTX_ROWS, 2 * channels), BF16), b, b, sds((VEC_ROWS, channels), F32)],
        scratch_shapes=[pltpu.VMEM(w.shape, BF16) for w in (out, qkv, conv2, conv1)]
        + [pltpu.VMEM((pixels + 2 * EDGE, 3 * channels), BF16), pltpu.VMEM((pixels, channels), BF16), pltpu.VMEM((pixels, channels), F32), pltpu.VMEM((pixels, channels), F32), pltpu.SemaphoreType.DMA((4,))],
        compiler_params=pltpu.CompilerParams(vmem_limit_bytes=48 << 20),
        name="backward_layer",
    )(g, v, vec, kvc, h, r, qkv_s, lse, out, qkv, conv2, conv1)


IMAGES_DEV = 2
SMALL_W, CONV2_W, CONV1_W = range(3)


def weights_kernel(section, *refs, parts):
    steps = parts[0]
    names = ("ot", "g", "n3t", "dqkv", "a2t", "db", "a1t", "dhb")
    src = {name: refs[n * steps : (n + 1) * steps] for n, name in enumerate(names)}
    refs = refs[len(names) * steps :]
    gout, gqkv, gconv2, gconv1 = refs[:4]
    held = dict(zip(names, refs[4 : 4 + len(names)]))
    field, buf, small, sems, out_sems = refs[4 + len(names) :]
    pixels, channels = held["g"].shape[1:]
    wide = 2 * LANES

    def copies(other):
        return [
            [pltpu.make_async_copy(src[name][step], held[name].at[slot], sems.at[slot, n]) for slot, step in enumerate((1, other))]
            for n, name in enumerate(names)
        ]

    first, last = copies(2), copies(0)
    is_first = section[0] == 0

    @pl.when(is_first)
    def _():
        for pair in first:
            for copy in pair:
                copy.start()

    @pl.when(jnp.logical_not(is_first))
    def _():
        for pair in last:
            for copy in pair:
                copy.start()

    zeros = jnp.zeros((EDGE, field.shape[2]), BF16)
    for slot in range(2):
        field[slot, 0:EDGE, :] = zeros
        field[slot, pixels + EDGE :, :] = zeros

    def ready(*wanted):
        for n, name in enumerate(names):
            if name in wanted:
                for copy in first[n]:
                    copy.wait()

    sent = []

    def ship(source, target):
        copy = pltpu.make_async_copy(source, target, out_sems.at[len(sent)])
        copy.start()
        sent.append(copy)

    ready("ot", "g")
    for lanes in range(0, channels, wide):
        cols = slice(lanes, lanes + wide)
        small[:, cols] = (nn(held["ot"][0], held["g"][0, :, cols]) + nn(held["ot"][1], held["g"][1, :, cols])).astype(BF16)
    ship(small.at[:, 0:channels], gout)
    ready("n3t", "dqkv")
    for lanes in range(0, 3 * channels, wide):
        cols = slice(lanes, lanes + wide)
        total = nn(held["n3t"][0], held["dqkv"][0, :, cols]) + nn(held["n3t"][1], held["dqkv"][1, :, cols])
        small[:, channels + lanes : channels + lanes + wide] = total.astype(BF16)
    ship(small.at[:, channels : 4 * channels], gqkv)
    for number, (left, right, target) in enumerate((("a2t", "db", gconv2), ("a1t", "dhb", gconv1))):
        ready(left, right)
        for slot in range(2):
            for lanes in range(0, channels, LANES):
                put_shifted(field.at[slot], lanes, held[right][slot, :, lanes : lanes + LANES].astype(F32))
        for row in range(3):
            for col in range(3):
                tap = row * 3 + col
                spot = number * 9 + tap
                for lanes in range(0, channels, wide):
                    at = slice((2 - col) * channels + lanes, (2 - col) * channels + lanes + wide)
                    down = slice((2 - row) * IMG, (2 - row) * IMG + pixels)
                    total = nn(held[left][0], field[0, down, at]) + nn(held[left][1], field[1, down, at])
                    buf[number, tap * channels : (tap + 1) * channels, lanes : lanes + wide] = total.astype(BF16)
                ship(buf.at[number, pl.ds(tap * channels, channels)], target.at[pl.ds(tap * channels, channels)])
    for copy in sent:
        copy.wait()


def weights_call(section, factors, channels):
    names = ("ot", "g", "n3t", "dqkv", "a2t", "db", "a1t", "dhb")
    steps = len(factors["g"])
    hbm = pl.BlockSpec(memory_space=pl.ANY)
    sds = jax.ShapeDtypeStruct
    pixels = factors["g"][0].shape[0]
    return pl.pallas_call(
        functools.partial(weights_kernel, parts=(steps,)),
        in_specs=[pl.BlockSpec(memory_space=pltpu.SMEM)] + [hbm] * (8 * steps),
        out_specs=[hbm] * 4,
        out_shape=[sds((channels, channels), BF16), sds((channels, 3 * channels), BF16), sds((9 * channels, channels), BF16), sds((9 * channels, channels), BF16)],
        scratch_shapes=[pltpu.VMEM((IMAGES_DEV,) + factors[name][0].shape, BF16) for name in names]
        + [pltpu.VMEM((IMAGES_DEV, pixels + 2 * EDGE, 3 * channels), BF16), pltpu.VMEM((2, 9 * channels, channels), BF16), pltpu.VMEM((channels, 4 * channels), BF16), pltpu.SemaphoreType.DMA((2, 8)), pltpu.SemaphoreType.DMA((20,))],
        compiler_params=pltpu.CompilerParams(vmem_limit_bytes=48 << 20),
        name="weight_gradients",
    )(section, *[one for name in names for one in factors[name]])


def passed_along(value, axis, steps):
    count = lax.axis_size(axis)
    first, last = (max(0, -steps), min(count, count - steps))
    return lax.ppermute(value, axis, [(source, source + steps) for source in range(first, last)])


def halved_sums(arrays, axis):
    count = lax.axis_size(axis)
    index = lax.axis_index(axis)
    bits = [1 << k for k in range(count.bit_length() - 1)]
    orders = (bits, bits[1::-1] + bits[2:], bits[2:] + bits[:2])
    state = []
    for number, array in enumerate(arrays):
        state.append((array, bits, orders[number % 3]))
    for step in range(len(bits)):
        held = []
        for array, left, order in state:
            bit = order[step]
            above = len([one for one in left if one > bit])
            view = array.reshape((1 << above, 2, array.shape[0] >> (above + 1)) + array.shape[1:])
            mine = (index // bit) % 2
            keep = lax.dynamic_index_in_dim(view, mine, 1, keepdims=False).astype(F32)
            send = lax.dynamic_index_in_dim(view, 1 - mine, 1, keepdims=False).astype(BF16)
            got = lax.ppermute(send, axis, [(one, one ^ bit) for one in range(count)])
            held.append((keep, got, [one for one in left if one != bit], order))
        state = [
            ((keep + got.astype(F32)).reshape((-1,) + keep.shape[2:]), left, order)
            for keep, got, left, order in held
        ]
    return [array[0] for array, left, order in state]


def two_parts(values):
    high = values.astype(BF16)
    return jnp.concatenate([high, (values - high.astype(F32)).astype(BF16)], axis=1)


MB = 2


def body(
    acts, present, embed, context,
    norm1_gain, norm1_bias, conv1_weight, conv1_bias, emb_weight, emb_bias, norm2_gain, norm2_bias,
    conv2_weight, conv2_bias, norm3_gain, norm3_bias, qkv_weight, context_weight, out_weight, out_bias,
):
    is_first = lax.axis_index("section") == 0
    section = lax.axis_index("section").astype(jnp.int32).reshape(1)
    images_dev, pixels, channels = acts.shape[1:]
    emb_width = embed.shape[1]
    extra_count = context.shape[1]
    wide = 2 * channels
    count = lax.axis_size("dp")
    conv1, conv2, qkv, out = conv1_weight[0], conv2_weight[0], qkv_weight[0], out_weight[0]
    source = acts[0]
    cotan = source * present.astype(BF16)[:, None, None]

    emb32 = embed.astype(F32)
    emb_act = (emb32 * jax.nn.sigmoid(emb32)).astype(BF16)
    modulation = nn(emb_act, emb_weight[0]) + emb_bias
    extra_kv = nn(context.reshape(-1, channels), context_weight[0]).astype(BF16)
    extra_kv = jnp.pad(
        extra_kv.reshape(images_dev, extra_count, wide), ((0, 0), (0, CTX_ROWS - extra_count), (0, 0))
    )
    rows = jnp.concatenate(
        [norm1_gain, norm1_bias, conv1_bias, norm2_gain, norm2_bias, conv2_bias, norm3_gain, norm3_bias, out_bias], axis=0
    )
    vecs = jnp.concatenate(
        [
            jnp.broadcast_to(rows[None], (images_dev,) + rows.shape),
            modulation.reshape(images_dev, 2, channels),
            jnp.zeros((images_dev, VEC_ROWS - rows.shape[0] - 2, channels), F32),
        ],
        axis=1,
    )

    def pick(array, first, second):
        return jnp.where(is_first, array[first], array[second])

    stash = []
    layers = []
    received = jnp.zeros((pixels, channels), BF16)
    for step in range(MB + 1):
        at = (min(step, MB - 1), max(step - 1, 0))
        layer_in = jnp.where(is_first, source[at[0]], received)
        vec, kvc = pick(vecs, *at), pick(extra_kv, *at)
        layer, sending, a1t, a2t, n3t, ot, h, r, qkv_s, lse = forward_call(
            layer_in, vec, kvc, conv1, conv2, qkv, out
        )
        stash.append((layer_in, vec, kvc, a1t, a2t, n3t, ot, h, r, qkv_s, lse))
        layers.append(layer)
        if step < MB:
            received = passed_along(sending, "section", 1)

    factors = {name: [] for name in ("ot", "g", "n3t", "dqkv", "a2t", "db", "a1t", "dhb")}
    results, vectors, d_extras = [], [], []
    back_recv = jnp.zeros((pixels, channels), BF16)
    for step in range(MB + 1):
        grad = jnp.where(is_first, back_recv, cotan[max(MB - 1 - step, 0)])
        layer_in, vec, kvc, a1t, a2t, n3t, ot, h, r, qkv_s, lse = stash[MB - step]
        sending, res, dqkv, dkvc, db, dhb, gv = backward_call(
            grad, layer_in, vec, kvc, h, r, qkv_s, lse, out, qkv, conv2, conv1
        )
        if step < MB:
            back_recv = passed_along(sending, "section", -1)
        for name, one in zip(factors, (ot, grad, n3t, dqkv, a2t, db, a1t, dhb)):
            factors[name].append(one)
        results.append(res)
        vectors.append(gv)
        d_extras.append(dkvc[:extra_count])
    gout, gqkv, gconv2, gconv1 = weights_call(section, factors, channels)

    mask = present.astype(F32)
    result = jnp.stack(
        [
            jnp.where(is_first, results[2], layers[1] * mask[0]),
            jnp.where(is_first, results[1], layers[2] * mask[1]),
        ]
    )[None]

    def by_shard(array):
        return array.reshape((count, array.shape[0] // count) + array.shape[1:])

    rest = jnp.concatenate([by_shard(gqkv), by_shard(gout)], axis=2)
    conv1_shard, conv2_shard, rest_shard = halved_sums(
        [by_shard(gconv1), by_shard(gconv2), rest], "dp"
    )
    emb_cols = emb_width // count
    context_cols = channels // count

    def split_columns(array, columns):
        return array.reshape(-1, count, columns).swapaxes(0, 1).reshape(count, -1)

    early = jnp.concatenate(
        [
            split_columns(emb_act, emb_cols),
            split_columns(context.reshape(-1, channels), context_cols),
        ],
        axis=1,
    )
    early = lax.all_to_all(early, "dp", 0, 0)
    emb_part = early[:, : images_dev * emb_cols].reshape(count * images_dev, emb_cols)
    context_part = early[:, images_dev * emb_cols :].reshape(-1, context_cols)
    d_mods = [gv[G_SCALE : G_SHIFT + 1].reshape(-1).astype(BF16) for gv in vectors]
    same = jnp.concatenate(
        [
            jnp.where(is_first, d_mods[2], d_mods[1]),
            jnp.where(is_first, d_mods[1], d_mods[0]),
            jnp.where(is_first, d_extras[2], d_extras[1]).reshape(-1),
            jnp.where(is_first, d_extras[1], d_extras[0]).reshape(-1),
        ]
    )
    vector = vectors[1] + jnp.where(is_first, vectors[2], vectors[0])
    each = channels // count
    vector = vector[:G_SCALE].reshape(G_SCALE, count, each).swapaxes(0, 1).reshape(count, -1)
    width = vector.shape[1]
    late = jnp.concatenate(
        [two_parts(vector), jnp.broadcast_to(same[None], (count, same.shape[0]))], axis=1
    )
    late = lax.all_to_all(late, "dp", 0, 0)
    summed = jnp.sum(late[:, : 2 * width].astype(F32), axis=0)
    summed = (summed[:width] + summed[width:]).reshape(G_SCALE, each)
    d_mod_g = late[:, 2 * width : 2 * width + images_dev * wide].reshape(-1, wide)
    d_extra_g = late[:, 2 * width + images_dev * wide :].reshape(-1, wide)
    emb_bias_all = jnp.sum(d_mod_g.astype(F32), axis=0)
    emb_bias_shard = lax.dynamic_slice_in_dim(
        emb_bias_all, lax.axis_index("dp") * (wide // count), wide // count, 0
    )
    shards = (
        summed[G_N1G], summed[G_N1B], conv1_shard, summed[G_C1B], tn(emb_part, d_mod_g), emb_bias_shard,
        summed[G_N2G], summed[G_N2B], conv2_shard, summed[G_C2B], summed[G_N3G], summed[G_N3B],
        rest_shard[:, : 3 * channels], tn(context_part, d_extra_g), rest_shard[:, 3 * channels :], summed[G_OB],
    )
    return (result,) + tuple(shard[None] for shard in shards)


def solution(mesh):
    in_specs = (
        P("section", "dp", None, None),
        P("dp"),
        P("dp", None),
        P("dp", None, None),
        P("section", None),
        P("section", None),
        P("section", None, None),
        P("section", None),
        P("section", None, None),
        P("section", None),
        P("section", None),
        P("section", None),
        P("section", None, None),
        P("section", None),
        P("section", None),
        P("section", None),
        P("section", None, None),
        P("section", None, None),
        P("section", None, None),
        P("section", None),
    )
    out_specs = (
        P("section", "dp", None, None),
        P("section", "dp"),
        P("section", "dp"),
        P("section", "dp", None),
        P("section", "dp"),
        P("section", "dp", None),
        P("section", "dp"),
        P("section", "dp"),
        P("section", "dp"),
        P("section", "dp", None),
        P("section", "dp"),
        P("section", "dp"),
        P("section", "dp"),
        P("section", "dp", None),
        P("section", "dp", None),
        P("section", "dp", None),
        P("section", "dp"),
    )
    return jax.shard_map(body, mesh=mesh, in_specs=in_specs, out_specs=out_specs, check_vma=False)
```

```python
import functools

import jax
import jax.numpy as jnp
from jax import lax
from jax.experimental import pallas as pl
from jax.experimental.pallas import tpu as pltpu
from jax.sharding import PartitionSpec as P

HEADS = 8
HEAD = 64
IMG = 16
EPSILON = 1e-05
MB = 2
LANES = 128
EDGE = IMG
CTX_ROWS = 16
VEC_ROWS = 16
GROUP = 4
PIECE = 32
VMEM_LIMIT = 64 << 20
COST = pl.CostEstimate(flops=1000, bytes_accessed=1000, transcendentals=0)
BF16 = jnp.bfloat16
F32 = jnp.float32
(N1G, N1B, C1B, N2G, N2B, C2B, N3G, N3B, OB, SCALE, SHIFT) = range(11)
NT = (((1,), (1,)), ((), ()))
TN = (((0,), (0,)), ((), ()))
VMEM = pl.BlockSpec(memory_space=pltpu.VMEM)
HBM = pl.BlockSpec(memory_space=pltpu.HBM)
SMEM = pl.BlockSpec(memory_space=pltpu.SMEM)
sds = jax.ShapeDtypeStruct


def nn(left, right):
    return jnp.dot(left, right, preferred_element_type=F32)


def nt(left, right):
    return lax.dot_general(left, right, NT, preferred_element_type=F32)


def tn(left, right):
    return lax.dot_general(left, right, TN, preferred_element_type=F32)


def group_sum(rows):
    lane = lax.broadcasted_iota(jnp.int32, rows.shape, 1)
    for step in (1, 2, 4, 8):
        above = pltpu.roll(rows, LANES - step, 1)
        below = pltpu.roll(rows, step, 1)
        rows = rows + jnp.where((lane & step) != 0, below, above)
    return rows


def column_sum(block):
    return jnp.sum(block, axis=0, keepdims=True)


def centre(block):
    count = block.shape[0] * 16
    mean = group_sum(column_sum(block)) * (1.0 / count)
    block = block - mean
    var = group_sum(column_sum(block * block)) * (1.0 / count)
    rstd = lax.rsqrt(var + EPSILON)
    return block * rstd, rstd


def scaled_back(xhat, rstd, dy, gain):
    count = xhat.shape[0] * 16
    d_gain = column_sum(dy * xhat)
    d_bias = column_sum(dy)
    both = group_sum(jnp.concatenate([d_bias * gain, d_gain * gain], axis=0)) * (1.0 / count)
    dx = rstd * (dy * gain - both[0:1] - xhat * both[1:2])
    return dx, d_gain, d_bias


def sigmoid(values):
    return 1.0 / (1.0 + jnp.exp(-values))


def shifted(block):
    column = lax.broadcasted_iota(jnp.int32, block.shape, 0) % IMG
    before = jnp.where(column == 0, 0.0, pltpu.roll(block, 1, 0))
    after = jnp.where(column == IMG - 1, 0.0, pltpu.roll(block, block.shape[0] - 1, 0))
    return before.astype(BF16), block.astype(BF16), after.astype(BF16)


def put_shifted(field, lanes, block):
    pixels, width = block.shape[0], field.shape[1] // 3
    for place, one in enumerate(shifted(block)):
        field[EDGE : EDGE + pixels, place * width + lanes : place * width + lanes + LANES] = one


def clear_edges(field):
    zeros = jnp.zeros((EDGE, field.shape[1]), BF16)
    field[0:EDGE, :] = zeros
    field[field.shape[0] - EDGE :, :] = zeros


def conv_of(field, weight, lanes, wide, pixels):
    depth = weight.shape[0] // 3
    total = None
    for row in range(3):
        part = nn(
            field[row * IMG : row * IMG + pixels, :],
            weight[row * depth : (row + 1) * depth, lanes : lanes + wide],
        )
        total = part if total is None else total + part
    return total


def conv_back(field, weight, lanes, wide, pixels):
    width = weight.shape[1]
    total = None
    for row in range(3):
        for col in range(3):
            tap = (row * 3 + col) * width
            part = nt(
                field[(2 - row) * IMG : (2 - row) * IMG + pixels, (2 - col) * width : (3 - col) * width],
                weight[tap + lanes : tap + lanes + wide, :],
            )
            total = part if total is None else total + part
    return total


class Copies:
    def __init__(self, sems):
        self.sems, self.used, self.open = sems, 0, []

    def make(self, source, target):
        copy = pltpu.make_async_copy(source, target, self.sems.at[self.used])
        self.used += 1
        return copy

    def start(self, source, target):
        copy = self.make(source, target)
        copy.start()
        self.open.append(copy)
        return copy

    def finish(self):
        for copy in self.open:
            copy.wait()
        self.open = []


def only_on(section, wanted, work):
    if wanted is None:
        work()
    else:
        pl.when(section == wanted)(work)


FORWARD_OUTS = ("layer", "send", "n3t", "ot", "h", "r", "qkv", "lse", "a1t", "a2t")


def forward_kernel(step, fuse, place, vecs, kvcs, *refs, names):
    ref = dict(zip(names, refs))
    conv1, conv2, qkvw, outw = (ref["s_" + name] for name in ("conv1", "conv2", "qkvw", "outw"))
    v_ref, field, act, o_ref = ref["s_v"], ref["s_field"], ref["s_act"], ref["s_o"]
    a1t, a2t, n3t, ot = ref["s_a1t"], ref["s_a2t"], ref["s_n3t"], ref["s_ot"]
    h_ref, r_ref, qkv_ref, lse_ref = ref["s_h"], ref["s_r"], ref["s_qkv"], ref["s_lse"]
    l_ref, send_ref = ref["s_layer"], ref["s_send"]
    pixels, channels = v_ref.shape
    blocks = [slice(n, n + LANES) for n in range(0, channels, LANES)]
    section = place[0]
    tokens = ref["tokens"]

    def work():
        loads, stores = Copies(ref["in_sems"]), Copies(ref["out_sems"])
        if step < MB:
            only_on(section, 0, lambda: loads.make(ref["acts"].at[step], v_ref).start())
            loads.used = 0
        if step > 0:
            only_on(section, 1, lambda: loads.make(ref["received"], v_ref).start())
            loads.used = 0
        v_wait = loads.make(ref["acts"].at[0], v_ref)
        waits = [loads.start(ref["conv1"], conv1)]
        image = step - section
        vec, kvc = vecs.at[image], kvcs.at[image]

        def ship(name, slot=None):
            target = ref[name] if slot is None else ref[name].at[slot]
            stores.start(ref["s_" + name], target)

        clear_edges(field)
        v_wait.wait()
        waits += [loads.start(ref[name], ref["s_" + name]) for name in ("conv2", "qkvw", "outw")]
        for at in blocks:
            xhat, _ = centre(v_ref[:, at].astype(F32))
            u = xhat * vec[N1G : N1G + 1, at] + vec[N1B : N1B + 1, at]
            a1 = u * sigmoid(u)
            put_shifted(field, at.start, a1)
            a1t[at, :] = a1.astype(BF16).T
        ship("a1t", 1 if fuse else None)
        waits[0].wait()
        wide = 2 * LANES
        for lanes in range(0, channels, wide):
            h_ref[:, lanes : lanes + wide] = (
                conv_of(field, conv1, lanes, wide, pixels) + vec[C1B : C1B + 1, lanes : lanes + wide]
            )
        ship("h")
        for at in blocks:
            xhat, _ = centre(h_ref[:, at])
            n = xhat * vec[N2G : N2G + 1, at] + vec[N2B : N2B + 1, at]
            u = n * (1.0 + vec[SCALE : SCALE + 1, at]) + vec[SHIFT : SHIFT + 1, at]
            a2 = u * sigmoid(u)
            put_shifted(field, at.start, a2)
            a2t[at, :] = a2.astype(BF16).T
        ship("a2t", 1 if fuse else None)
        waits[1].wait()
        for lanes in range(0, channels, wide):
            r_ref[:, lanes : lanes + wide] = (
                conv_of(field, conv2, lanes, wide, pixels) + vec[C2B : C2B + 1, lanes : lanes + wide]
            ) + v_ref[:, lanes : lanes + wide].astype(F32)
        ship("r")
        for at in blocks:
            xhat, _ = centre(r_ref[:, at])
            n3 = (xhat * vec[N3G : N3G + 1, at] + vec[N3B : N3B + 1, at]).astype(BF16)
            act[:, at] = n3
            n3t[at, :] = n3.T
        ship("n3t")
        waits[2].wait()
        for lanes in range(0, 3 * channels, wide):
            part = nn(act[...], qkvw[:, lanes : lanes + wide])
            if lanes < channels:
                part = part.astype(BF16).astype(F32) * HEAD ** (-0.5)
            qkv_ref[:, lanes : lanes + wide] = part.astype(BF16)
        ship("qkv")
        lane = lax.broadcasted_iota(jnp.int32, (pixels, LANES), 1)
        token = lax.broadcasted_iota(jnp.int32, (CTX_ROWS, pixels), 0)
        zero = jnp.zeros((pixels, LANES), BF16)
        for pair, at in enumerate(blocks):
            at_v = slice(channels + at.start, channels + at.stop)
            q2 = qkv_ref[:, at]
            k2 = qkv_ref[:, channels + at.start : channels + at.stop]
            v2t = qkv_ref[:, 2 * channels + at.start : 2 * channels + at.stop].T
            kc, vc = kvc[:, at], kvc[:, at_v]
            for half in range(2):
                head = 2 * pair + half
                qm = jnp.where((lane >= HEAD) == (half == 1), q2, zero)
                s = nt(k2, qm)
                sc = jnp.where(token < tokens, nt(kc, qm), -jnp.inf)
                top = jnp.maximum(jnp.max(s, axis=0, keepdims=True), jnp.max(sc, axis=0, keepdims=True))
                e, ec = jnp.exp(s - top), jnp.exp(sc - top)
                total = column_sum(e) + column_sum(ec)
                lse_ref[head : head + 1, :] = top + jnp.log(total)
                share = 1.0 / total
                p, pc = (e * share).astype(BF16), (ec * share).astype(BF16)
                rows = slice(half * HEAD, (half + 1) * HEAD)
                o = nn(v2t[rows, :], p) + tn(vc, pc)[rows, :]
                ot[head * HEAD : (head + 1) * HEAD, :] = o.astype(BF16)
            o_ref[:, at] = ot[at, :].T
        ship("ot")
        ship("lse")
        waits[3].wait()
        for lanes in range(0, channels, wide):
            cols = slice(lanes, lanes + wide)
            layer = nn(o_ref[...], outw[:, cols]) + vec[OB : OB + 1, cols] + r_ref[:, cols]
            l_ref[:, cols] = layer
            send_ref[:, cols] = (layer + v_ref[:, cols].astype(F32)).astype(BF16)
        ship("layer")
        ship("send")
        stores.finish()

    if fuse:
        packs = Copies(ref["pack_sems"])
        passed = ("a1t_1", "a2t_1", "a1t_0", "a2t_0")
        for name in passed:
            packs.start(ref[name], ref["s_" + name])
    only_on(section, {0: 0, MB: 1}.get(step), work)
    if fuse:
        packs.finish()
        for name in passed[:2]:
            packs.start(ref["s_" + name], ref[name[:3]].at[0])

        def earlier():
            more = Copies(ref["pack_sems"])
            for name in passed[2:]:
                more.start(ref["s_" + name], ref[name[:3]].at[1])
            more.finish()

        only_on(section, 0, earlier)
        packs.finish()


def forward_call(step, place, vecs, kvcs, acts, received, weights, tokens, earlier=None):
    pixels, channels = acts.shape[1:]
    fuse = earlier is not None
    conv1, conv2, qkv, out = weights
    ins = {"acts": acts}
    if step > 0:
        ins["received"] = received
    ins.update(conv1=conv1, conv2=conv2, qkvw=qkv, outw=out)
    if fuse:
        for n, (a1t, a2t) in enumerate(earlier):
            ins["a1t_%d" % n], ins["a2t_%d" % n] = a1t, a2t
    tr, b, f = ((channels, pixels), BF16), ((pixels, channels), BF16), ((pixels, channels), F32)
    held = dict(
        layer=f, send=b, n3t=tr, ot=tr, h=f, r=f, qkv=((pixels, 3 * channels), BF16), lse=((HEADS, pixels), F32), a1t=tr, a2t=tr
    )
    outs = {name: held[name] for name in FORWARD_OUTS}
    if fuse:
        outs["a1t"] = outs["a2t"] = ((MB,) + tr[0], BF16)
    scratch = {"s_" + name: pltpu.VMEM(*held[name]) for name in FORWARD_OUTS}
    for name in ("conv1", "conv2", "qkvw", "outw"):
        scratch["s_" + name] = pltpu.VMEM(ins[name].shape, BF16)
    scratch["s_v"] = scratch["s_act"] = scratch["s_o"] = pltpu.VMEM(*b)
    scratch["s_field"] = pltpu.VMEM((pixels + 2 * EDGE, 3 * channels), BF16)
    scratch["in_sems"] = pltpu.SemaphoreType.DMA((5,))
    scratch["out_sems"] = pltpu.SemaphoreType.DMA((len(outs),))
    if fuse:
        for name in ("a1t_1", "a2t_1", "a1t_0", "a2t_0"):
            scratch["s_" + name] = pltpu.VMEM(*tr)
    scratch["pack_sems"] = pltpu.SemaphoreType.DMA((8,))
    names = list(ins) + list(outs) + list(scratch)

    def kernel(place, vecs, kvcs, *refs):
        forward_kernel(step, fuse, place, vecs, kvcs, *refs, tokens, names=names + ["tokens"])

    result = pl.pallas_call(
        kernel,
        in_specs=[SMEM, VMEM, VMEM] + [HBM] * len(ins),
        out_specs=[HBM] * len(outs),
        out_shape=[sds(*one) for one in outs.values()],
        scratch_shapes=list(scratch.values()),
        compiler_params=pltpu.CompilerParams(vmem_limit_bytes=VMEM_LIMIT),
        cost_estimate=COST,
        name="forward_layer",
    )(place, vecs, kvcs, *ins.values())
    return dict(zip(outs, result))


(G_N1G, G_N1B, G_C1B, G_N2G, G_N2B, G_C2B, G_N3G, G_N3B, G_OB, G_SCALE, G_SHIFT) = range(11)
BACKWARD_OUTS = ("send", "res", "dqkv", "g", "dbq", "dhbq")


def backward_kernel(step, fuse, place, present, vecs, kvcs, *refs, names):
    ref = dict(zip(names, refs))
    gv, dkvc_ref = ref["gv"], ref["dkvc"]
    conv1, conv2, qkvw, outw = (ref["s_" + name] for name in ("conv1", "conv2", "qkvw", "outw"))
    h_ref, r_ref, qkv_ref, lse_ref = ref["s_h"], ref["s_r"], ref["s_qkv"], ref["s_lse"]
    v_ref, g_ref, field, d_o, dr, tmp = (ref["s_" + name] for name in ("v", "g", "field", "d_o", "dr", "tmp"))
    send_ref, res_ref, dqkv_ref, dbq, dhbq = (ref["s_" + name] for name in ("send", "res", "dqkv", "dbq", "dhbq"))
    pixels, channels = v_ref.shape
    blocks = [slice(n, n + LANES) for n in range(0, channels, LANES)]
    wide = 2 * LANES
    section, low, high = place[0], place[1], place[2]
    tokens = ref["tokens"]

    def parts(name, source, stores, slot):
        mine = low if name == "dbq" else high
        for n in range(GROUP):
            stores.start(source.at[mine ^ n], ref["%s_to%d" % (name, n)].at[slot])

    def work():
        loads, stores = Copies(ref["in_sems"]), Copies(ref["out_sems"])
        image = MB - step - section
        slab, other = ref["s_slab"], ref["s_other"]
        slab_wait = loads.start(ref["acts"].at[image], slab)
        if step > 0:
            only_on(section, 0, lambda: loads.make(ref["grad"], other).start())
            loads.used = 1
        if step < MB:
            only_on(section, 1, lambda: loads.make(ref["received"], other).start())
            loads.used = 1
        other_wait = loads.make(ref["acts"].at[0], other)
        waits = {}

        def fetch(*wanted):
            for name in wanted:
                waits[name] = loads.start(ref[name], ref["s_" + name])

        fetch("outw", "qkv", "lse")
        vec, kvc = vecs.at[image], kvcs.at[image]

        def ship(name):
            stores.start(ref["s_" + name], ref[name])

        clear_edges(field)
        gv[...] = jnp.zeros(gv.shape, F32)
        slab_wait.wait()
        other_wait.wait()
        shown = present[image].astype(F32)
        for at in blocks:
            first, second = slab[:, at], other[:, at]
            v_ref[:, at] = jnp.where(section == 0, first, second)
            g = jnp.where(section == 0, second.astype(F32), first.astype(F32) * shown)
            g_ref[:, at] = g.astype(BF16)
            gv[G_OB : G_OB + 1, at] = column_sum(g)
        ship("g")
        waits["outw"].wait()
        fetch("qkvw", "r")
        for lanes in range(0, channels, wide):
            d_o[:, lanes : lanes + wide] = nt(g_ref[...], outw[lanes : lanes + wide, :]).astype(BF16)
        lane = lax.broadcasted_iota(jnp.int32, (pixels, LANES), 1)
        token = lax.broadcasted_iota(jnp.int32, (CTX_ROWS, pixels), 0)
        zero = jnp.zeros((pixels, LANES), BF16)
        waits["qkv"].wait()
        waits["lse"].wait()
        fetch("conv2", "h", "conv1")
        for pair, at in enumerate(blocks):
            at_v = slice(channels + at.start, channels + at.stop)
            at_vv = slice(2 * channels + at.start, 2 * channels + at.stop)
            q2, do2 = qkv_ref[:, at], d_o[:, at]
            k2, v2 = qkv_ref[:, at_v], qkv_ref[:, at_vv]
            kc, vc = kvc[:, at], kvc[:, at_v]
            k2t = k2.T
            dk = dv = dkc = dvc = None
            dqt = []
            for half in range(2):
                head = 2 * pair + half
                mine = (lane >= HEAD) == (half == 1)
                qm, dom = jnp.where(mine, q2, zero), jnp.where(mine, do2, zero)
                lse = lse_ref[head : head + 1, :]
                p = jnp.exp(nt(k2, qm) - lse)
                pc = jnp.exp(jnp.where(token < tokens, nt(kc, qm), -jnp.inf) - lse)
                dp, dpc = nt(v2, dom), nt(vc, dom)
                dot = column_sum(p * dp) + column_sum(pc * dpc)
                ds, dsc = (p * (dp - dot)).astype(BF16), (pc * (dpc - dot)).astype(BF16)
                pb, pcb = p.astype(BF16), pc.astype(BF16)
                rows = slice(half * HEAD, (half + 1) * HEAD)
                dqt.append((nn(k2t[rows, :], ds) + tn(kc, dsc)[rows, :]) * HEAD ** (-0.5))
                four = (nn(ds, qm), nn(pb, dom), nn(dsc, qm), nn(pcb, dom))
                if half == 0:
                    dk, dv, dkc, dvc = four
                else:
                    dk, dv, dkc, dvc = dk + four[0], dv + four[1], dkc + four[2], dvc + four[3]
            dqkv_ref[:, at] = jnp.concatenate(dqt, axis=0).astype(BF16).T
            dqkv_ref[:, at_v] = dk.astype(BF16)
            dqkv_ref[:, at_vv] = dv.astype(BF16)
            dkvc_ref[:, at] = dkc.astype(BF16)
            dkvc_ref[:, at_v] = dvc.astype(BF16)
        ship("dqkv")
        waits["qkvw"].wait()
        for lanes in range(0, channels, wide):
            tmp[:, lanes : lanes + wide] = nt(dqkv_ref[...], qkvw[lanes : lanes + wide, :])
        waits["r"].wait()
        for n, at in enumerate(blocks):
            xhat, rstd = centre(r_ref[:, at])
            dx, d_gain, d_bias = scaled_back(xhat, rstd, tmp[:, at], vec[N3G : N3G + 1, at])
            gv[G_N3G : G_N3G + 1, at] = d_gain
            gv[G_N3B : G_N3B + 1, at] = d_bias
            total = g_ref[:, at].astype(F32) + dx
            dr[:, at] = total
            rounded = total.astype(BF16)
            dbq[n] = rounded
            rounded = rounded.astype(F32)
            gv[G_C2B : G_C2B + 1, at] = column_sum(rounded)
            put_shifted(field, at.start, rounded)
        if fuse:
            parts("dbq", dbq, stores, 1)
        else:
            ship("dbq")
        waits["conv2"].wait()
        for lanes in range(0, channels, wide):
            tmp[:, lanes : lanes + wide] = conv_back(field, conv2, lanes, wide, pixels)
        waits["h"].wait()
        for n, at in enumerate(blocks):
            xhat, rstd = centre(h_ref[:, at])
            gain, bias = vec[N2G : N2G + 1, at], vec[N2B : N2B + 1, at]
            more = 1.0 + vec[SCALE : SCALE + 1, at]
            u = (xhat * gain + bias) * more + vec[SHIFT : SHIFT + 1, at]
            s = sigmoid(u)
            du = tmp[:, at] * (s * (1.0 + u * (1.0 - s)))
            dx, d_gain, d_bias = scaled_back(xhat, rstd, du, gain * more)
            gv[G_SHIFT : G_SHIFT + 1, at] = d_bias
            gv[G_SCALE : G_SCALE + 1, at] = d_gain * gain + d_bias * bias
            gv[G_N2G : G_N2G + 1, at] = d_gain * more
            gv[G_N2B : G_N2B + 1, at] = d_bias * more
            rounded = dx.astype(BF16)
            dhbq[n] = rounded
            rounded = rounded.astype(F32)
            gv[G_C1B : G_C1B + 1, at] = column_sum(rounded)
            put_shifted(field, at.start, rounded)
        if fuse:
            parts("dhbq", dhbq, stores, 1)
        else:
            ship("dhbq")
        waits["conv1"].wait()
        for lanes in range(0, channels, wide):
            tmp[:, lanes : lanes + wide] = conv_back(field, conv1, lanes, wide, pixels)
        for at in blocks:
            xhat, rstd = centre(v_ref[:, at].astype(F32))
            gain = vec[N1G : N1G + 1, at]
            u = xhat * gain + vec[N1B : N1B + 1, at]
            s = sigmoid(u)
            du = tmp[:, at] * (s * (1.0 + u * (1.0 - s)))
            dx, d_gain, d_bias = scaled_back(xhat, rstd, du, gain)
            gv[G_N1G : G_N1G + 1, at] = d_gain
            gv[G_N1B : G_N1B + 1, at] = d_bias
            total = dr[:, at] + dx
            send_ref[:, at] = total.astype(BF16)
            res_ref[:, at] = total + g_ref[:, at].astype(F32)
        if step < MB:
            ship("send")
        if fuse:
            stores.start(res_ref, ref["res"].at[0])
        elif step > 0:
            ship("res")
        stores.finish()

    if fuse:
        packs = Copies(ref["pack_sems"])
        passed = ("dbq_1", "dhbq_1", "dbq_0", "dhbq_0")
        for name in passed:
            packs.start(ref[name], ref["s_" + name])

        def fetch_first():
            one = Copies(ref["pack_sems"])
            one.used = 4
            one.make(ref["res_1"], ref["s_given_1"]).start()

        def fetch_second():
            two = Copies(ref["pack_sems"])
            two.used = 4
            two.make(ref["layer_2"], ref["s_given_1"]).start()
            two.start(ref["layer_1"], ref["s_given_0"]).wait()

        only_on(section, 0, fetch_first)
        only_on(section, 1, fetch_second)
        packs.open.append(packs.make(ref["layer_2"], ref["s_given_1"]))
    only_on(section, {0: 1, MB: 0}.get(step), work)
    if fuse:
        packs.finish()
        for name in passed[:2]:
            parts(name[:-2], ref["s_" + name], packs, 0)

        def earlier():
            more = Copies(ref["pack_sems"])
            more.used = 6 + 2 * GROUP
            for name in passed[2:]:
                parts(name[:-2], ref["s_" + name], more, 1)
            for slot in range(MB):
                shown = present[slot].astype(F32)
                for at in blocks:
                    ref["s_given_%d" % slot][:, at] = ref["s_given_%d" % slot][:, at] * shown
            more.start(ref["s_given_0"], ref["res"].at[0])
            more.finish()

        only_on(section, 1, earlier)
        packs.start(ref["s_given_1"], ref["res"].at[1]).wait()
        packs.open.pop()
        packs.finish()


def backward_call(step, place, present, vecs, kvcs, acts, received, grad, kept, weights, tokens, earlier=None, given=None, after=()):
    pixels, channels = acts.shape[1:]
    fuse = earlier is not None
    conv1, conv2, qkv, out = weights
    ins = {"acts": acts}
    if step > 0:
        ins["grad"] = grad
    if step < MB:
        ins["received"] = received
    ins.update({name: kept[name] for name in ("h", "r", "qkv", "lse")})
    ins.update(outw=out, qkvw=qkv, conv2=conv2, conv1=conv1)
    if fuse:
        for n, (dbq, dhbq) in enumerate(earlier):
            ins["dbq_%d" % n], ins["dhbq_%d" % n] = dbq, dhbq
        ins.update(given)
    ins.update({"after_%d" % n: one for n, one in enumerate(after)})
    b, f = ((pixels, channels), BF16), ((pixels, channels), F32)
    quarters = ((channels // LANES, pixels, LANES), BF16)
    held = dict(send=b, res=f, dqkv=((pixels, 3 * channels), BF16), g=b, dbq=quarters, dhbq=quarters)
    outs = {"dqkv": held["dqkv"], "g": b}
    if step < MB:
        outs["send"] = b
    if step > 0:
        outs["res"] = ((MB,) + f[0], F32) if fuse else f
    if fuse:
        for name in ("dbq", "dhbq"):
            for n in range(GROUP):
                outs["%s_to%d" % (name, n)] = ((MB, pixels, LANES), BF16)
    else:
        outs.update(dbq=quarters, dhbq=quarters)
    small = {"gv": ((VEC_ROWS, channels), F32), "dkvc": ((CTX_ROWS, 2 * channels), BF16)}
    scratch = {"s_" + name: pltpu.VMEM(*held[name]) for name in BACKWARD_OUTS}
    for name in ("h", "r", "qkv", "lse", "outw", "qkvw", "conv2", "conv1"):
        scratch["s_" + name] = pltpu.VMEM(ins[name].shape, ins[name].dtype)
    for name in ("v", "slab", "other", "d_o"):
        scratch["s_" + name] = pltpu.VMEM(*b)
    scratch["s_dr"] = scratch["s_tmp"] = pltpu.VMEM(*f)
    scratch["s_field"] = pltpu.VMEM((pixels + 2 * EDGE, 3 * channels), BF16)
    scratch["in_sems"] = pltpu.SemaphoreType.DMA((10,))
    scratch["out_sems"] = pltpu.SemaphoreType.DMA((len(outs) + 2,))
    if fuse:
        for name in ("dbq_1", "dhbq_1", "dbq_0", "dhbq_0"):
            scratch["s_" + name] = pltpu.VMEM(*quarters)
        for name in ("given_0", "given_1"):
            scratch["s_" + name] = pltpu.VMEM(*f)
    scratch["pack_sems"] = pltpu.SemaphoreType.DMA((8 + 4 * GROUP,))
    names = list(ins) + list(small) + list(outs) + list(scratch)

    def kernel(place, present, vecs, kvcs, *refs):
        backward_kernel(step, fuse, place, present, vecs, kvcs, *refs, tokens, names=names + ["tokens"])

    result = pl.pallas_call(
        kernel,
        in_specs=[SMEM, SMEM, VMEM, VMEM] + [HBM] * len(ins),
        out_specs=[VMEM] * len(small) + [HBM] * len(outs),
        out_shape=[sds(*one) for one in list(small.values()) + list(outs.values())],
        scratch_shapes=list(scratch.values()),
        compiler_params=pltpu.CompilerParams(vmem_limit_bytes=VMEM_LIMIT),
        cost_estimate=COST,
        name="backward_layer",
    )(place, present, vecs, kvcs, *ins.values())
    return dict(zip(list(small) + list(outs), result))


BLOCK_ROWS = 16
VECTOR_ROWS = 3


def shares_kernel(place, gv_0, gv_1, gv_2, dkvc_0, dkvc_1, dkvc_2, emb, ctx, *refs, names, tokens):
    ref = dict(zip(names, refs))
    section = place[0]
    shards, block, rows = ref["s_shards"], ref["s_block"], ref["s_rows"]
    channels = gv_1.shape[1]
    wide = 2 * LANES

    loads, stores = Copies(ref["in_sems"]), Copies(ref["out_sems"])
    waits = {}
    for n, name in enumerate(("ot", "g", "n3t", "dqkv")):
        held = ref["s_" + name]
        waits[name] = [loads.start(ref[name + "_1"], held.at[0])]
        for wanted, step in ((0, MB), (1, 0)):

            def fetch():
                one = Copies(ref["in_sems"])
                one.used = 2 * n + 1
                one.make(ref["%s_%d" % (name, step)], held.at[1]).start()

            only_on(section, wanted, fetch)
        waits[name].append(loads.make(ref[name + "_1"], held.at[1]))
    first = section == 0
    gv_b = jnp.where(first, gv_2[...], gv_0[...])
    dkvc_b = jnp.where(first, dkvc_2[...].astype(F32), dkvc_0[...].astype(F32))

    rows[...] = jnp.zeros(rows.shape, F32)
    after = 1 + tokens + VECTOR_ROWS
    for slot, (vector, kv) in enumerate(((gv_1, dkvc_1), (gv_b, dkvc_b))):
        at = 2 * channels * slot
        rows[0:1, at : at + channels] = vector[G_SCALE : G_SCALE + 1]
        rows[0:1, at + channels : at + 2 * channels] = vector[G_SHIFT : G_SHIFT + 1]
        rows[1 : 1 + tokens, at : at + 2 * channels] = kv[0:tokens].astype(F32)
        image = jnp.where(first, 1 - slot, slot)
        rows[after + slot : after + slot + 1, :] = emb[image].astype(F32)
        for token in range(tokens):
            at = token * channels
            rows[after + MB + slot : after + MB + slot + 1, at : at + channels] = ctx[image, token : token + 1].astype(F32)
    for n in range(G_SCALE):
        at = channels * (n % GROUP)
        row = 1 + tokens + n // GROUP
        rows[row : row + 1, at : at + channels] = gv_1[n : n + 1] + gv_b[n : n + 1]
    for n in range(rows.shape[1] // LANES):
        block[n // 2, (n % 2) * BLOCK_ROWS : (n % 2 + 1) * BLOCK_ROWS, :] = rows[:, n * LANES : (n + 1) * LANES].astype(BF16)
    each = shards.shape[2]
    for n in range(GROUP):
        stores.start(block, ref["out"].at[n, pl.ds(GROUP * each, block.shape[0])])

    def product(left, right, spot):
        for wait in waits[left] + waits[right]:
            wait.wait()
        left, right = ref["s_" + left], ref["s_" + right]
        for lanes in range(0, right.shape[2], wide):
            cols = slice(lanes, lanes + wide)
            total = (nn(left[0], right[0, :, cols]) + nn(left[1], right[1, :, cols])).astype(BF16)
            for shard in range(GROUP * GROUP):
                for k in range(2):
                    piece = total[shard * PIECE : (shard + 1) * PIECE, k * LANES : (k + 1) * LANES]
                    shards[shard // GROUP, shard % GROUP, spot + lanes // LANES + k] = piece

    product("ot", "g", 3 * channels // LANES)
    product("n3t", "dqkv", 0)
    for n in range(GROUP):
        for line in range(GROUP):
            stores.start(shards.at[line, n], ref["out"].at[n, pl.ds(line * each, each)])
    stores.finish()


def call(kernel, place, small, ins, outs, scratch, name, flops=10**8, bytes_accessed=4 * 10**6, after=(), **given):
    ins = dict(ins, **{"after_%d" % n: one for n, one in enumerate(after)})
    names = list(ins) + list(outs) + list(scratch)

    def run(place, *refs):
        kernel(place, *refs, names=names, **given)

    result = pl.pallas_call(
        run,
        in_specs=[SMEM] + [VMEM] * len(small) + [HBM] * len(ins),
        out_specs=[HBM] * len(outs),
        out_shape=[sds(*one) for one in outs.values()],
        scratch_shapes=list(scratch.values()),
        compiler_params=pltpu.CompilerParams(vmem_limit_bytes=VMEM_LIMIT),
        cost_estimate=COST,
        name=name,
    )(place, *small, *ins.values())
    return dict(zip(outs, result))


def shares_call(place, small, factors, tokens, after):
    channels = small[0].shape[1]
    pixels = factors["g"][0].shape[0]
    pieces = 4 * channels // LANES
    extra = 4 * channels * BLOCK_ROWS // (LANES * PIECE)
    ins = {"%s_%d" % (name, n): one for name, arrays in factors.items() for n, one in enumerate(arrays)}
    outs = {"out": ((GROUP, GROUP * pieces + extra, PIECE, LANES), BF16)}
    scratch = {"s_" + name: pltpu.VMEM((MB,) + arrays[1].shape, BF16) for name, arrays in factors.items()}
    scratch["s_shards"] = pltpu.VMEM((GROUP, GROUP, pieces, PIECE, LANES), BF16)
    scratch["s_block"] = pltpu.VMEM((extra, PIECE, LANES), BF16)
    scratch["s_rows"] = pltpu.VMEM((BLOCK_ROWS, 4 * channels), F32)
    scratch["in_sems"] = pltpu.SemaphoreType.DMA((8,))
    scratch["out_sems"] = pltpu.SemaphoreType.DMA((GROUP * (GROUP + 1),))
    return call(
        shares_kernel, place, small, ins, outs, scratch, "shares", 4 * MB * 2 * pixels * channels * channels,
        after=after, tokens=tokens,
    )["out"]


def conv_weights_kernel(place, *refs, names):
    ref = dict(zip(names, refs))
    low, high = place[1], place[2]
    loads, stores = Copies(ref["in_sems"]), Copies(ref["out_sems"])
    taps = ref["s_taps"]
    channels, depth = ref["s_left2"].shape
    pixels = depth // (GROUP * MB)
    each = 9 * channels // (GROUP * GROUP)
    waits = {}
    for which in (2, 1):
        left, right = ref["s_left%d" % which], ref["s_right%d" % which]
        for n in range(GROUP):
            for image in range(MB):
                spot = n * MB + image
                waits[which, spot] = loads.start(ref["d%d_%d" % (which, n)].at[image], right.at[spot])
        for n in range(GROUP):
            for image in range(MB):
                spot = n * MB + image
                source = ref["a1"].at[high ^ n, image] if which == 1 else ref["a2_%d" % n].at[image]
                waits[which, GROUP * MB + spot] = loads.start(source, left.at[:, pl.ds(spot * pixels, pixels)])
    for which in (2, 1):
        left, right, result = (ref["s_%s%d" % (name, which)] for name in ("left", "right", "result"))
        for spot in range(GROUP * MB):
            waits[which, spot].wait()
            start = spot * pixels
            for col, one in enumerate(reversed(shifted(right[spot].astype(F32)))):
                for row in range(3):
                    at = slice((3 * row + col) * LANES, (3 * row + col + 1) * LANES)
                    move = (row - 1) * IMG
                    if move > 0:
                        taps[start : start + move, at] = jnp.zeros((move, LANES), BF16)
                        taps[start + move : start + pixels, at] = one[: pixels - move]
                    elif move < 0:
                        taps[start : start + pixels + move, at] = one[-move:]
                        taps[start + pixels + move : start + pixels, at] = jnp.zeros((-move, LANES), BF16)
                    else:
                        taps[start : start + pixels, at] = one
        for spot in range(GROUP * MB):
            waits[which, GROUP * MB + spot].wait()
        for tap in range(0, 9, 2):
            count = min(2, 9 - tap)
            total = nn(left[...], taps[:, tap * LANES : (tap + count) * LANES]).astype(BF16)
            for k in range(count):
                result[(tap + k) * channels : (tap + k + 1) * channels, :] = total[:, k * LANES : (k + 1) * LANES]
        for n in range(GROUP):
            if which == 2:
                start = pl.multiple_of((high ^ n) * GROUP * each, PIECE)
                stores.start(result.at[pl.ds(start, GROUP * each)], ref[("keep", "away")[n % 2]].at[n // 2])
            else:
                for line in range(GROUP):
                    start = pl.multiple_of((GROUP * line + (low ^ n)) * each, PIECE)
                    stores.start(result.at[pl.ds(start, each)], ref["to%d" % n].at[line])
    stores.finish()


def conv_weights_call(place, a2, d2, a1, d1, after):
    channels, pixels = a1.shape[-2:]
    each = 9 * channels // (GROUP * GROUP)
    ins = {"a1": a1}
    ins.update({"a2_%d" % n: one for n, one in enumerate(a2)})
    ins.update({"d2_%d" % n: one for n, one in enumerate(d2)})
    ins.update({"d1_%d" % n: one for n, one in enumerate(d1)})
    outs = {"to%d" % n: ((GROUP, each, LANES), BF16) for n in range(GROUP)}
    outs.update({name: ((2, GROUP * each, LANES), BF16) for name in ("keep", "away")})
    images = GROUP * MB
    scratch = {"s_taps": pltpu.VMEM((images * pixels, 9 * LANES), BF16)}
    for which in (1, 2):
        scratch["s_left%d" % which] = pltpu.VMEM((channels, images * pixels), BF16)
        scratch["s_right%d" % which] = pltpu.VMEM((images, pixels, LANES), BF16)
        scratch["s_result%d" % which] = pltpu.VMEM((9 * channels, LANES), BF16)
    scratch["in_sems"] = pltpu.SemaphoreType.DMA((4 * images,))
    scratch["out_sems"] = pltpu.SemaphoreType.DMA((GROUP * (GROUP + 1),))
    return call(conv_weights_kernel, place, [], ins, outs, scratch, "conv_weights", after=after)


def halves_kernel(place, keep, got, *refs, names):
    ref = dict(zip(names, refs))
    stores = Copies(ref["out_sems"])
    for slot, name in ((1, "away"), (0, "own")):
        ref["s_" + name][...] = (keep[slot].astype(F32) + got[slot].astype(F32)).astype(BF16)
        stores.start(ref["s_" + name], ref[name])
    stores.finish()


def halves_call(place, keep, got):
    shape = keep.shape[1:]
    return call(
        halves_kernel, place, [keep, got], {}, {name: (shape, BF16) for name in ("own", "away")},
        {"s_own": pltpu.VMEM(shape, BF16), "s_away": pltpu.VMEM(shape, BF16), "out_sems": pltpu.SemaphoreType.DMA((2,))}, "halves",
    )


def quarters_kernel(place, *refs, names):
    parts, refs = refs[:2], refs[2:]
    ref = dict(zip(names, refs))
    low = place[1]
    stores, total = Copies(ref["out_sems"]), ref["s_total"]
    each = total.shape[1]
    for line in range(GROUP):
        terms = [one[line * each : (line + 1) * each].astype(F32) for one in parts]
        total[line] = (terms[0] + terms[1]).astype(BF16)
    for n in range(GROUP):
        stores.start(total.at[low ^ n], ref["to%d" % n])
    stores.finish()


def quarters_call(place, parts, after):
    shape = (parts[0].shape[0] // GROUP, LANES)
    return call(
        quarters_kernel, place, list(parts), {}, {"to%d" % n: (shape, BF16) for n in range(GROUP)},
        {"s_total": pltpu.VMEM((GROUP,) + shape, BF16), "out_sems": pltpu.SemaphoreType.DMA((GROUP,))}, "quarters", after=after,
    )


def gated(value, after):
    def kernel(*refs):
        pass

    return pl.pallas_call(
        kernel,
        in_specs=[HBM] * (1 + len(after)),
        out_specs=HBM,
        out_shape=sds(value.shape, value.dtype),
        input_output_aliases={0: 0},
        compiler_params=pltpu.CompilerParams(vmem_limit_bytes=VMEM_LIMIT, has_side_effects=True),
        cost_estimate=COST,
        name="gate",
    )(value, *after)


def plane_kernel(place, *refs, names, tokens):
    ref = dict(zip(names, refs))
    low = place[1]
    loads, stores = Copies(ref["in_sems"]), Copies(ref["out_sems"])
    total, rows, block, shares = ref["s_total"], ref["s_rows"], ref["s_block"], ref["s_shares"]
    waits = [loads.start(ref["share"], shares)]
    pieces = ref["s_pieces"]
    more = [loads.start(ref["piece%d" % n], pieces.at[n]) for n in range(GROUP)]
    for wait in waits:
        wait.wait()
    each = total.shape[1]
    for line in range(GROUP):
        for k in range(each):
            parts = [shares[n, line * each + k].astype(F32) for n in range(GROUP)]
            total[line, k] = (parts[0] + parts[1] + parts[2] + parts[3]).astype(BF16)
    gather = 1 + tokens
    after = gather + VECTOR_ROWS
    blocks = rows.shape[0]
    few = ref["s_few"]
    rows[...] = jnp.zeros(rows.shape, F32)
    few[...] = jnp.zeros(few.shape, F32)
    per_token = blocks // tokens
    for k in range(blocks):
        sums = None
        for n in range(GROUP):
            part = shares[n, GROUP * each + k // 2, (k % 2) * BLOCK_ROWS : (k % 2 + 1) * BLOCK_ROWS, :].astype(F32)
            rows[k, n * gather : (n + 1) * gather, :] = part[:gather]
            few[k, MB * n : MB * (n + 1), :] = part[after : after + MB]
            for slot in range(MB):
                row = (n * MB + slot) * tokens + k // per_token
                few[blocks + k % per_token, row : row + 1, :] = part[after + MB + slot : after + MB + slot + 1]
            part = part[gather:after]
            sums = part if sums is None else sums + part
        rows[k, GROUP * gather : GROUP * gather + VECTOR_ROWS, :] = sums
        block[k] = rows[k].astype(BF16)
    ref["s_thin"][...] = few[...].astype(BF16)
    for wait in more:
        wait.wait()
    conv = ref["s_conv"]
    for line in range(GROUP):
        for k in range(conv.shape[1]):
            parts = [pieces[n, line, k * PIECE : (k + 1) * PIECE, :].astype(F32) for n in range(GROUP)]
            conv[line, k] = (parts[0] + parts[1] + parts[2] + parts[3]).astype(BF16)
    for n in range(GROUP):
        target = ref["out"].at[n]
        stores.start(conv.at[n], target.at[pl.ds(each + blocks + 2, conv.shape[1])])
        stores.start(total.at[n], target.at[pl.ds(0, each)])
        stores.start(block, target.at[pl.ds(each, blocks)])
        stores.start(ref["s_thin"].at[n * GROUP + low], target.at[each + blocks])
        stores.start(ref["s_thin"].at[blocks + n], target.at[each + blocks + 1])
    stores.finish()


def plane_call(place, shares, pieces, channels, tokens, after):
    each = blocks = 4 * channels // LANES
    per_token = blocks // tokens
    lines = pieces[0].shape[1]
    ins = {"share": shares}
    ins.update({"piece%d" % n: one for n, one in enumerate(pieces)})
    outs = {"out": ((GROUP, each + blocks + 2 + lines // PIECE, PIECE, LANES), BF16)}
    scratch = {
        "s_shares": pltpu.VMEM(shares.shape, BF16),
        "s_pieces": pltpu.VMEM((GROUP,) + pieces[0].shape, BF16),
        "s_conv": pltpu.VMEM((GROUP, lines // PIECE, PIECE, LANES), BF16),
        "s_total": pltpu.VMEM((GROUP, each, PIECE, LANES), BF16),
        "s_rows": pltpu.VMEM((blocks, PIECE, LANES), F32),
        "s_few": pltpu.VMEM((blocks + per_token, PIECE, LANES), F32),
        "s_block": pltpu.VMEM((blocks, PIECE, LANES), BF16),
        "s_thin": pltpu.VMEM((blocks + per_token, PIECE, LANES), BF16),
        "in_sems": pltpu.SemaphoreType.DMA((2 * GROUP,)),
        "out_sems": pltpu.SemaphoreType.DMA((5 * GROUP,)),
    }
    return call(plane_kernel, place, [], ins, outs, scratch, "plane_sums", after=after, tokens=tokens)["out"]


def last_kernel(place, *refs, names, tokens, channels):
    lines, quarters, refs = [refs[0].at[n] for n in range(GROUP)], refs[1 : 1 + GROUP], refs[1 + GROUP :]
    ref = dict(zip(names, refs))
    low = place[1]
    stores = Copies(ref["out_sems"])

    def ship(name):
        stores.start(ref["s_" + name], ref[name])

    each = blocks = 4 * channels // LANES
    for n in range(GROUP):
        at = slice(n * LANES, (n + 1) * LANES)
        for k in range(ref["s_conv1"].shape[0] // PIECE):
            ref["s_conv1"][k * PIECE : (k + 1) * PIECE, at] = lines[n][each + blocks + 2 + k].astype(F32)
        at = pl.ds(pl.multiple_of((low ^ n) * LANES, LANES), LANES)
        ref["s_conv2"][:, at] = quarters[n][...].astype(F32)
    ship("conv1")
    ship("conv2")
    for k in range(each):
        parts = [one[k].astype(F32) for one in lines]
        total = parts[0] + parts[1] + parts[2] + parts[3]
        name = "qkv" if k < 3 * channels // LANES else "out"
        at = k * LANES if name == "qkv" else k * LANES - 3 * channels
        ref["s_" + name][:, at : at + LANES] = total
    ship("qkv")
    ship("out")
    wide = 2 * channels // LANES
    gather = 1 + tokens
    left = ref["s_left"]
    left[...] = jnp.zeros(left.shape, F32)
    for n in range(GROUP):
        for k in range(blocks):
            start = (2 * n + k // wide) * PIECE
            at = (k % wide) * LANES
            ref["s_d"][start : start + PIECE, at : at + LANES] = lines[n][each + k]
        emb = lines[n][each + blocks].astype(F32)
        ctx = lines[n][each + blocks + 1].astype(F32)
        for source in range(GROUP):
            for slot in range(MB):
                row = (2 * n + slot) * PIECE + source * gather
                spot = source * MB + slot
                left[row : row + 1, 0:LANES] = emb[spot : spot + 1]
                left[row + 1 : row + gather, LANES : 2 * LANES] = ctx[spot * tokens : (spot + 1) * tokens]
                left[row : row + 1, 2 * LANES :] = jnp.ones((1, LANES), F32)
    product = tn(left[...].astype(BF16), ref["s_d"][...])
    ref["s_emb"][...] = product[:LANES]
    ref["s_all"][...] = product[LANES : 2 * LANES]
    width = ref["s_ctx"].shape[0]
    ref["s_ctx"][...] = ref["s_all"][pl.ds(pl.multiple_of(low * width, width), width), :]
    ship("emb")
    ship("ctx")
    vec = ref["s_vec"]
    vec[...] = jnp.zeros(vec.shape, F32)
    for k in range(2):
        vec[G_SCALE + k : G_SCALE + k + 1, :] = product[2 * LANES : 2 * LANES + 1, k * channels : (k + 1) * channels]
    at = GROUP * gather
    for k in range(blocks):
        parts = [one[each + k].astype(F32) for one in lines]
        total = parts[0] + parts[1] + parts[2] + parts[3]
        for row in range(VECTOR_ROWS):
            spot = row * GROUP + k // (channels // LANES)
            if spot < G_SCALE:
                lanes = (k % (channels // LANES)) * LANES
                vec[spot : spot + 1, lanes : lanes + LANES] = total[at + row : at + row + 1]
    ship("vec")
    stores.finish()


def last_call(place, lines, quarters, channels, tokens, emb_cols, context_cols):
    outs = {
        "conv1": ((quarters[0].shape[0], channels), F32),
        "conv2": ((quarters[0].shape[0], channels), F32),
        "qkv": ((PIECE, 3 * channels), F32),
        "out": ((PIECE, channels), F32),
        "emb": ((emb_cols, 2 * channels), F32),
        "ctx": ((context_cols, 2 * channels), F32),
        "vec": ((VEC_ROWS, channels), F32),
    }
    scratch = {"s_" + name: pltpu.VMEM(*one) for name, one in outs.items()}
    scratch["s_d"] = pltpu.VMEM((2 * GROUP * PIECE, 2 * channels), BF16)
    scratch["s_left"] = pltpu.VMEM((2 * GROUP * PIECE, 3 * LANES), F32)
    scratch["s_all"] = pltpu.VMEM((LANES, 2 * channels), F32)
    scratch["out_sems"] = pltpu.SemaphoreType.DMA((len(outs),))
    return call(last_kernel, place, [lines] + list(quarters), {}, outs, scratch, "last_sums", tokens=tokens, channels=channels)


def weights_kernel(place, *refs, steps):
    names = ("ot", "g", "n3t", "dqkv", "a2t", "db", "a1t", "dhb")
    src = {name: refs[n * steps : (n + 1) * steps] for n, name in enumerate(names)}
    refs = refs[len(names) * steps :]
    gout, gqkv, gconv2, gconv1 = refs[:4]
    held = dict(zip(names, refs[4 : 4 + len(names)]))
    field, buf, small, sems, out_sems = refs[4 + len(names) :]
    pixels, channels = held["g"].shape[1:]
    wide = 2 * LANES

    def copies(other):
        return [
            [pltpu.make_async_copy(src[name][step], held[name].at[slot], sems.at[slot, n]) for slot, step in enumerate((1, other))]
            for n, name in enumerate(names)
        ]

    first, last = copies(2), copies(0)

    def go(pairs):
        for pair in pairs:
            for copy in pair:
                copy.start()

    only_on(place[0], 0, lambda: go(first))
    only_on(place[0], 1, lambda: go(last))
    for slot in range(MB):
        clear_edges(field.at[slot])

    def ready(*wanted):
        for n, name in enumerate(names):
            if name in wanted:
                for copy in first[n]:
                    copy.wait()

    stores = Copies(out_sems)
    ready("ot", "g")
    for lanes in range(0, channels, wide):
        cols = slice(lanes, lanes + wide)
        small[:, cols] = (nn(held["ot"][0], held["g"][0, :, cols]) + nn(held["ot"][1], held["g"][1, :, cols])).astype(BF16)
    stores.start(small.at[:, 0:channels], gout)
    ready("n3t", "dqkv")
    for lanes in range(0, 3 * channels, wide):
        cols = slice(lanes, lanes + wide)
        total = nn(held["n3t"][0], held["dqkv"][0, :, cols]) + nn(held["n3t"][1], held["dqkv"][1, :, cols])
        small[:, channels + lanes : channels + lanes + wide] = total.astype(BF16)
    stores.start(small.at[:, channels : 4 * channels], gqkv)
    for number, (left, right, target) in enumerate((("a2t", "db", gconv2), ("a1t", "dhb", gconv1))):
        ready(left, right)
        for slot in range(MB):
            for lanes in range(0, channels, LANES):
                put_shifted(field.at[slot], lanes, held[right][slot, :, lanes : lanes + LANES].astype(F32))
        for row in range(3):
            for col in range(3):
                tap = row * 3 + col
                for lanes in range(0, channels, wide):
                    at = slice((2 - col) * channels + lanes, (2 - col) * channels + lanes + wide)
                    down = slice((2 - row) * IMG, (2 - row) * IMG + pixels)
                    total = nn(held[left][0], field[0, down, at]) + nn(held[left][1], field[1, down, at])
                    buf[number, tap * channels : (tap + 1) * channels, lanes : lanes + wide] = total.astype(BF16)
                rows = pl.ds(tap * channels, channels)
                stores.start(buf.at[number, rows], target.at[rows])
    stores.finish()


def weights_call(place, factors, channels):
    names = ("ot", "g", "n3t", "dqkv", "a2t", "db", "a1t", "dhb")
    steps = len(factors["g"])
    pixels = factors["g"][0].shape[0]
    return pl.pallas_call(
        functools.partial(weights_kernel, steps=steps),
        in_specs=[SMEM] + [HBM] * (8 * steps),
        out_specs=[HBM] * 4,
        out_shape=[sds((channels, channels), BF16), sds((channels, 3 * channels), BF16), sds((9 * channels, channels), BF16), sds((9 * channels, channels), BF16)],
        scratch_shapes=[pltpu.VMEM((MB,) + factors[name][0].shape, BF16) for name in names]
        + [pltpu.VMEM((MB, pixels + 2 * EDGE, 3 * channels), BF16), pltpu.VMEM((2, 9 * channels, channels), BF16), pltpu.VMEM((channels, 4 * channels), BF16), pltpu.SemaphoreType.DMA((2, 8)), pltpu.SemaphoreType.DMA((20,))],
        compiler_params=pltpu.CompilerParams(vmem_limit_bytes=VMEM_LIMIT),
        name="weight_gradients",
    )(place, *[one for name in names for one in factors[name]])


def halved_sums(arrays, axis):
    count = lax.axis_size(axis)
    index = lax.axis_index(axis)
    bits = [1 << k for k in range(count.bit_length() - 1)]
    orders = (bits, bits[1::-1] + bits[2:], bits[2:] + bits[:2])
    state = [(array, bits, orders[number % 3]) for number, array in enumerate(arrays)]
    for step in range(len(bits)):
        held = []
        for array, left, order in state:
            bit = order[step]
            above = len([one for one in left if one > bit])
            view = array.reshape((1 << above, 2, array.shape[0] >> (above + 1)) + array.shape[1:])
            mine = (index // bit) % 2
            keep = lax.dynamic_index_in_dim(view, mine, 1, keepdims=False).astype(F32)
            send = lax.dynamic_index_in_dim(view, 1 - mine, 1, keepdims=False).astype(BF16)
            got = lax.ppermute(send, axis, [(one, one ^ bit) for one in range(count)])
            held.append((keep, got, [one for one in left if one != bit], order))
        state = [
            ((keep + got.astype(F32)).reshape((-1,) + keep.shape[2:]), left, order)
            for keep, got, left, order in held
        ]
    return [array[0] for array, left, order in state]


def two_parts(values):
    high = values.astype(BF16)
    return jnp.concatenate([high, (values - high.astype(F32)).astype(BF16)], axis=1)


def late_in_general(is_first, place, factors, steps, context, emb_act, extra_count):
    count = lax.axis_size("dp")
    images_dev, emb_width = emb_act.shape
    channels = context.shape[-1]
    wide = 2 * channels

    def whole(quarters):
        return quarters.swapaxes(0, 1).reshape(quarters.shape[1], channels)

    factors = dict(factors, db=[whole(one["dbq"]) for one in steps], dhb=[whole(one["dhbq"]) for one in steps])
    gout, gqkv, gconv2, gconv1 = weights_call(place, factors, channels)

    def by_shard(array):
        return array.reshape((count, array.shape[0] // count) + array.shape[1:])

    rest = jnp.concatenate([by_shard(gqkv), by_shard(gout)], axis=2)
    conv1_shard, conv2_shard, rest_shard = halved_sums([by_shard(gconv1), by_shard(gconv2), rest], "dp")
    emb_cols = emb_width // count
    context_cols = channels // count

    def split_columns(array, columns):
        return array.reshape(-1, count, columns).swapaxes(0, 1).reshape(count, -1)

    early = jnp.concatenate(
        [split_columns(emb_act, emb_cols), split_columns(context.reshape(-1, channels), context_cols)], axis=1
    )
    early = lax.all_to_all(early, "dp", 0, 0)
    emb_part = early[:, : images_dev * emb_cols].reshape(count * images_dev, emb_cols)
    context_part = early[:, images_dev * emb_cols :].reshape(-1, context_cols)
    d_mods = [one["gv"][G_SCALE : G_SHIFT + 1].reshape(-1).astype(BF16) for one in steps]
    d_extras = [one["dkvc"][:extra_count].reshape(-1) for one in steps]
    same = jnp.concatenate(
        [
            jnp.where(is_first, d_mods[2], d_mods[1]),
            jnp.where(is_first, d_mods[1], d_mods[0]),
            jnp.where(is_first, d_extras[2], d_extras[1]),
            jnp.where(is_first, d_extras[1], d_extras[0]),
        ]
    )
    vector = steps[1]["gv"] + jnp.where(is_first, steps[2]["gv"], steps[0]["gv"])
    each = channels // count
    vector = vector[:G_SCALE].reshape(G_SCALE, count, each).swapaxes(0, 1).reshape(count, -1)
    width = vector.shape[1]
    late = jnp.concatenate([two_parts(vector), jnp.broadcast_to(same[None], (count, same.shape[0]))], axis=1)
    late = lax.all_to_all(late, "dp", 0, 0)
    summed = jnp.sum(late[:, : 2 * width].astype(F32), axis=0)
    summed = (summed[:width] + summed[width:]).reshape(G_SCALE, each)
    d_mod_g = late[:, 2 * width : 2 * width + images_dev * wide].reshape(-1, wide)
    d_extra_g = late[:, 2 * width + images_dev * wide :].reshape(-1, wide)
    emb_bias_all = jnp.sum(d_mod_g.astype(F32), axis=0)
    emb_bias = lax.dynamic_slice_in_dim(emb_bias_all, lax.axis_index("dp") * (wide // count), wide // count, 0)
    return (
        summed, emb_bias, conv1_shard, conv2_shard, rest_shard[:, : 3 * channels], rest_shard[:, 3 * channels :],
        tn(emb_part, d_mod_g), tn(context_part, d_extra_g),
    )


def partners(value, part, n, section=None):
    move = n if part == "low" else n * GROUP
    count = lax.axis_size("dp")
    if section is None:
        return lax.ppermute(value, "dp", [(one, one ^ move) for one in range(count)])
    pairs = [(2 * one + section, 2 * (one ^ move) + section) for one in range(count)]
    return lax.ppermute(value, ("dp", "section"), pairs)


def exchanged(values, part, section=None):
    return [values[0]] + [partners(values[n], part, n, section) for n in range(1, GROUP)]


def body(
    acts, present, embed, context,
    norm1_gain, norm1_bias, conv1_weight, conv1_bias, emb_weight, emb_bias, norm2_gain, norm2_bias,
    conv2_weight, conv2_bias, norm3_gain, norm3_bias, qkv_weight, context_weight, out_weight, out_bias,
):
    is_first = lax.axis_index("section") == 0
    count = lax.axis_size("dp")
    index = lax.axis_index("dp")
    place = jnp.stack([lax.axis_index("section"), index % GROUP, index // GROUP, 0]).astype(jnp.int32)
    images_dev, pixels, channels = acts.shape[1:]
    emb_width = embed.shape[1]
    tokens = context.shape[1]
    wide = 2 * channels
    weights = (conv1_weight[0], conv2_weight[0], qkv_weight[0], out_weight[0])
    grouped = count == GROUP * GROUP
    slab = acts[0]

    emb32 = embed.astype(F32)
    emb_act = (emb32 * jax.nn.sigmoid(emb32)).astype(BF16)
    modulation = nn(emb_act, emb_weight[0]) + emb_bias
    extra_kv = nn(context.reshape(-1, channels), context_weight[0]).astype(BF16)
    kvcs = jnp.pad(extra_kv.reshape(images_dev, tokens, wide), ((0, 0), (0, CTX_ROWS - tokens), (0, 0)))
    rows = jnp.concatenate(
        [norm1_gain, norm1_bias, conv1_bias, norm2_gain, norm2_bias, conv2_bias, norm3_gain, norm3_bias, out_bias], axis=0
    )
    vecs = jnp.concatenate(
        [
            jnp.broadcast_to(rows[None], (images_dev,) + rows.shape),
            modulation.reshape(images_dev, 2, channels),
            jnp.zeros((images_dev, VEC_ROWS - rows.shape[0] - 2, channels), F32),
        ],
        axis=1,
    )

    kept, arrived = [], [None]
    for step in range(MB + 1):
        earlier = [(one["a1t"], one["a2t"]) for one in kept] if grouped and step == MB else None
        kept.append(forward_call(step, place, vecs, kvcs, slab, arrived[step], weights, tokens, earlier))
        if step < MB:
            arrived.append(lax.ppermute(kept[step]["send"], "section", [(0, 1)]))
    if grouped:
        together = [[low + GROUP * high for high in range(GROUP)] for low in range(GROUP)]
        apart = [[low + GROUP * high for low in range(GROUP)] for high in range(GROUP)]
        a1_line = lax.all_gather(kept[MB]["a1t"], "dp", axis_index_groups=together)
        a2_plane = exchanged([kept[MB]["a2t"]] * GROUP, "low")

    steps, grad = [], None
    for step in range(MB + 1):
        f = MB - step
        more = {}
        if grouped and step == MB:
            more["earlier"] = [(one["dbq"], one["dhbq"]) for one in steps]
            more["given"] = {"res_1": steps[1]["res"], "layer_1": kept[1]["layer"], "layer_2": kept[2]["layer"]}
            more["after"] = a2_plane[1:]
        steps.append(backward_call(step, place, present, vecs, kvcs, slab, arrived[f], grad, kept[f], weights, tokens, **more))
        if step < MB:
            grad = lax.ppermute(steps[step]["send"], "section", [(1, 0)])

    each = channels // count
    factors = {
        "ot": [kept[MB - step]["ot"] for step in range(MB + 1)],
        "g": [one["g"] for one in steps],
        "n3t": [kept[MB - step]["n3t"] for step in range(MB + 1)],
        "dqkv": [one["dqkv"] for one in steps],
    }
    if grouped:
        last = steps[MB]
        result = last["res"]
        d2 = exchanged([last["dbq_to%d" % n] for n in range(GROUP)], "low")
        d1 = exchanged([last["dhbq_to%d" % n] for n in range(GROUP)], "high")
        small = [one["gv"] for one in steps] + [one["dkvc"] for one in steps] + [emb_act[:, None], context]
        own = shares_call(place, small, factors, tokens, [])
        own = gated(own, d2[1:] + d1[1:])
        shares = lax.all_to_all(own, "dp", 0, 0, axis_index_groups=apart)
        conv = conv_weights_call(place, a2_plane, d2, a1_line, d1, [own])
        got = partners(conv["away"], "high", 1)
        pieces = exchanged([conv["to%d" % n] for n in range(GROUP)], "low")
        halves = halves_call(place, conv["keep"], got)
        got = partners(halves["away"], "high", 2)
        plane = plane_call(place, shares, pieces, channels, tokens, [halves["own"]])
        lines = lax.all_to_all(plane, "dp", 0, 0, axis_index_groups=together)
        quarters = quarters_call(place, [halves["own"], got], [plane])
        quarters = exchanged([quarters["to%d" % n] for n in range(GROUP)], "low")
        end = last_call(place, lines, quarters, channels, tokens, emb_width // count, channels // count)
        vec = end["vec"]
        summed = lax.dynamic_slice_in_dim(vec[:G_SCALE], index * each, each, 1)
        bias = lax.dynamic_slice_in_dim(vec[G_SCALE : G_SHIFT + 1].reshape(-1), index * 2 * each, 2 * each, 0)
        conv1_shard, conv2_shard, qkv_shard, out_shard, emb_shard, ctx_shard = (
            end[name] for name in ("conv1", "conv2", "qkv", "out", "emb", "ctx")
        )
    else:
        mask = present.astype(F32)
        result = jnp.stack(
            [
                jnp.where(is_first, steps[2]["res"], kept[1]["layer"] * mask[0]),
                jnp.where(is_first, steps[1]["res"], kept[2]["layer"] * mask[1]),
            ]
        )
        late = late_in_general(
            is_first, place,
            dict(factors, a2t=[kept[MB - n]["a2t"] for n in range(MB + 1)], a1t=[kept[MB - n]["a1t"] for n in range(MB + 1)]),
            steps, context, emb_act, tokens,
        )
        summed, bias, conv1_shard, conv2_shard, qkv_shard, out_shard, emb_shard, ctx_shard = late
    shards = (
        summed[G_N1G], summed[G_N1B], conv1_shard, summed[G_C1B], emb_shard, bias, summed[G_N2G], summed[G_N2B],
        conv2_shard, summed[G_C2B], summed[G_N3G], summed[G_N3B], qkv_shard, ctx_shard, out_shard, summed[G_OB],
    )
    return (result[None],) + tuple(shard[None] for shard in shards)


def solution(mesh):
    in_specs = (
        P("section", "dp", None, None),
        P("dp"),
        P("dp", None),
        P("dp", None, None),
        P("section", None),
        P("section", None),
        P("section", None, None),
        P("section", None),
        P("section", None, None),
        P("section", None),
        P("section", None),
        P("section", None),
        P("section", None, None),
        P("section", None),
        P("section", None),
        P("section", None),
        P("section", None, None),
        P("section", None, None),
        P("section", None, None),
        P("section", None),
    )
    out_specs = (
        P("section", "dp", None, None),
        P("section", "dp"),
        P("section", "dp"),
        P("section", "dp", None),
        P("section", "dp"),
        P("section", "dp", None),
        P("section", "dp"),
        P("section", "dp"),
        P("section", "dp"),
        P("section", "dp", None),
        P("section", "dp"),
        P("section", "dp"),
        P("section", "dp"),
        P("section", "dp", None),
        P("section", "dp", None),
        P("section", "dp", None),
        P("section", "dp"),
    )
    return jax.shard_map(body, mesh=mesh, in_specs=in_specs, out_specs=out_specs, check_vma=False)
```
